256 devices in a mesh: dp: 8 (over x, core), blk: 32 (over y, z).
Axes of the slice: x: 4, y: 4, z: 8, core: 2. Of those that a mesh axis runs over, the one named last changes fastest.
Arguments:
- activations: bfloat16 [8192, 4096], P('dp', 'blk'), may hold values from -6 to 6
- out_grads: bfloat16 [8192, 8192], P('dp', 'blk'), may hold values from -0.0625 to 0.0625
- weight: bfloat16 [8, 32, 2, 256, 256], P('dp', 'blk'), may hold values from -6 to 6
- moment: float32 [8, 32, 2, 256, 256], P('dp', 'blk'), may hold values from -4 to 4
- second: float32 [8, 32, 2, 256, 256], P('dp', 'blk'), may hold values from 0.05 to 2
- left_gram: float32 [8, 32, 2, 256, 256], P('dp', 'blk'), as said below
- right_gram: float32 [8, 32, 2, 256, 256], P('dp', 'blk'), as said below
- left_basis: float32 [8, 32, 2, 256, 256], P('dp', 'blk'), as said below
- right_basis: float32 [8, 32, 2, 256, 256], P('dp', 'blk'), as said below
- slot_map: int32 [8, 32, 2], P('dp', 'blk'), may hold values from 0 to 1, each once within a row
- stale_mark: int32 [8, 32, 2], P('dp', 'blk'), may hold values from 0 to 1, as said below
Outputs:
- weight_new: bfloat16 [8, 32, 2, 256, 256], P('dp', 'blk')
- moment_new: float32 [8, 32, 2, 256, 256], P('dp', 'blk')
- second_new: float32 [8, 32, 2, 256, 256], P('dp', 'blk')
- left_new: float32 [8, 32, 2, 256, 256], P('dp', 'blk')
- right_new: float32 [8, 32, 2, 256, 256], P('dp', 'blk')
- left_basis_new: float32 [8, 32, 2, 256, 256], P('dp', 'blk')
- right_basis_new: float32 [8, 32, 2, 256, 256], P('dp', 'blk')
The draws below stay inside these ranges and needn't reach their ends.
Inputs may be any that keep to these rules, and one draw needn't show every extreme that they name: `left_gram`: each block is symmetric and positive definite. `right_gram`: each block is symmetric and positive definite. `left_basis`: each block is an orthogonal matrix. `right_basis`: each block is an orthogonal matrix. `stale_mark`: all 2 blocks of one owner carry the same mark.
All inputs are finite; a program needn't handle non-finite values.
Results may differ from the reference program's by a relative error of at most 0.009.
Values may be sent and summed in bfloat16 or wider, within the bound.
A program may use at most 128 MiB of HBM per device.

```python
import math
import jax
import jax.numpy as jnp
from jax import lax

B = 256
BPD = 2
TOK_DEV = 1024
TOKENS = 8192
ACT_COLS = 4096
OUT_COLS = 8192
N_DP = 8
N_BLK = 32


def symmetric_gram(key):
    key_rough, key_level = jax.random.split(key)
    full_shape = (N_DP, N_BLK, BPD, B, B)
    rough_part = jax.random.uniform(key_rough, full_shape, jnp.float32, -0.02, 0.02)
    mirror = rough_part + jnp.swapaxes(rough_part, -1, -2)
    levels = jnp.exp(jax.random.uniform(key_level, full_shape[:-1], jnp.float32, 0.0, math.log(8.0)))
    diagonal_mask = jnp.arange(B)[:, None] == jnp.arange(B)[None, :]
    return jnp.where(diagonal_mask, levels[..., None], mirror)


def orthogonal_blocks(key):
    key_order, key_sign = jax.random.split(key)
    block_count = N_DP * N_BLK * BPD
    indices = jnp.arange(B, dtype=jnp.float32)
    cosine = jnp.cos(math.pi * (indices[:, None] + 0.5) * indices[None, :] / B) * math.sqrt(2.0 / B)
    cosine = jnp.where(indices[None, :] == 0.0, cosine / math.sqrt(2.0), cosine)
    orders = jax.vmap(lambda subkey: jax.random.permutation(subkey, B))(jax.random.split(key_order, block_count))
    picked = jnp.transpose(jnp.take(cosine, orders, axis=1), (1, 0, 2))
    sign_flip = (jax.random.randint(key_sign, (block_count, 1, B), 0, 2) * 2 - 1).astype(jnp.float32)
    return (picked * sign_flip).reshape(N_DP, N_BLK, BPD, B, B)


def draw_left_gram(key, part):
    key = jax.random.fold_in(key, 5)
    return symmetric_gram(key)


def draw_right_gram(key, part):
    key = jax.random.fold_in(key, 6)
    return symmetric_gram(key)


def draw_left_basis(key, part):
    key = jax.random.fold_in(key, 7)
    return orthogonal_blocks(key)


def draw_right_basis(key, part):
    key = jax.random.fold_in(key, 8)
    return orthogonal_blocks(key)


def draw_stale_mark(key, part):
    key = jax.random.fold_in(key, 9)
    owner_count = N_DP * N_BLK
    order = jax.random.permutation(key, owner_count)
    flags = (order < max(1, owner_count // 4)).astype(jnp.int32).reshape(N_DP, N_BLK, 1)
    return jnp.broadcast_to(flags, (N_DP, N_BLK, BPD)).astype(jnp.int32)


def level_of(key, shape, cuts, low, top_value):
    level, own = 1.0, jax.random.fold_in(key, 6)
    for dim, parts in cuts:
        steps = jnp.exp(jax.random.uniform(jax.random.fold_in(own, dim), (parts,), jnp.float32, low / len(cuts), top_value / len(cuts)))
        level = level * jnp.repeat(steps, shape[dim] // parts).reshape([-1 if axis == dim else 1 for axis in range(len(shape))])
    return level


def noise(rng, dims, scale, limit, cuts=(), held_as=jnp.bfloat16):
    drawn = scale * jax.random.normal(rng, dims, jnp.float32)
    if cuts:
        drawn = drawn * level_of(rng, dims, cuts, -0.22, 0.18)
    return jnp.clip(drawn, -limit, limit).astype(held_as)


def setup_inputs(seed: int = 0) -> dict:
    seeds = jax.random.split(jax.random.key(seed), 12)
    activations = noise(seeds[0], (TOKENS, ACT_COLS), 1.0, 6.0, ((0, 8), (1, 32)))
    out_grads = noise(seeds[1], (TOKENS, OUT_COLS), TOKENS ** -0.5, 0.0625, ((0, 8), (1, 32)))
    weight = noise(seeds[2], (N_DP, N_BLK, BPD, B, B), 1.0, 6.0, ((0, 8), (1, 32)))
    moment = noise(seeds[3], (N_DP, N_BLK, BPD, B, B), 0.5, 4.0, ((0, 8), (1, 32)), jnp.float32)
    second = jnp.clip(jnp.exp(math.log(2.0) - 3.6888794 * jax.random.uniform(seeds[4], (N_DP, N_BLK, BPD, B, B), jnp.float32) ** level_of(seeds[4], (N_DP, N_BLK, BPD, B, B), ((0, 8), (1, 32)), -0.2, 0.2)), 0.05, 2.0)
    left_gram = draw_left_gram(jax.random.fold_in(seeds[11], 71), 0)
    right_gram = draw_right_gram(jax.random.fold_in(seeds[11], 71), 0)
    left_basis = draw_left_basis(jax.random.fold_in(seeds[11], 71), 0)
    right_basis = draw_right_basis(jax.random.fold_in(seeds[11], 71), 0)
    slot_map = jax.vmap(lambda own: jax.random.permutation(own, BPD))(jax.random.split(seeds[9], N_DP * N_BLK)).reshape((N_DP, N_BLK, BPD)).astype(jnp.int32)
    stale_mark = draw_stale_mark(jax.random.fold_in(seeds[11], 71), 0)
    return {"activations": activations, "out_grads": out_grads, "weight": weight, "moment": moment, "second": second, "left_gram": left_gram, "right_gram": right_gram, "left_basis": left_basis, "right_basis": right_basis, "slot_map": slot_map, "stale_mark": stale_mark}


highest = lax.Precision.HIGHEST
beta_one = 0.9
beta_two = 0.95
gram_beta = 0.95
eps_adam = 1e-08
learn_rate = 0.1
decay_rate = 0.01
bias_one = 1.0 - 0.9 ** 10
bias_two = 1.0 - 0.95 ** 10

def matmul(left, right):
    return jnp.dot(left.astype(jnp.float32), right.astype(jnp.float32), precision=highest, preferred_element_type=jnp.float32)

def gram_of(matrix):
    return lax.dot_general(matrix.astype(jnp.float32), matrix.astype(jnp.float32), (((0,), (0,)), ((), ())), precision=highest, preferred_element_type=jnp.float32)

def finish_basis(powered):
    inner_gram = gram_of(powered)
    factor = jnp.linalg.cholesky(inner_gram)
    return lax.linalg.triangular_solve(factor, powered, left_side=False, lower=True, transpose_a=True)

def refresh_basis(gram, basis):
    return finish_basis(matmul(gram, basis))

def soap_update(gradient, weight, moment, second, left_gram, right_gram, left_basis, right_basis):
    inverse_rows = 1.0 / gradient.shape[0]
    left_new = gram_beta * left_gram + (1.0 - gram_beta) * inverse_rows * matmul(gradient, gradient.T)
    right_new = gram_beta * right_gram + (1.0 - gram_beta) * inverse_rows * gram_of(gradient)
    moment_new = beta_one * moment + (1.0 - beta_one) * gradient
    rotated = matmul(matmul(left_basis.T, gradient), right_basis)
    second_new = beta_two * second + (1.0 - beta_two) * rotated * rotated
    turned = matmul(matmul(left_basis.T, moment_new), right_basis)
    normal = turned / bias_one / (jnp.sqrt(second_new / bias_two) + eps_adam)
    update = matmul(matmul(left_basis, normal), right_basis.T)
    weight_wide = weight.astype(jnp.float32)
    weight_new = (weight_wide - learn_rate * (update + decay_rate * weight_wide)).astype(jnp.bfloat16)
    return (weight_new, moment_new, second_new, left_new, right_new)

def block_step(entries):
    gradient, weight, moment, second, left_gram, right_gram, left_basis, right_basis, stale_flag = entries
    weight_new, moment_new, second_new, left_new, right_new = soap_update(gradient, weight, moment, second, left_gram, right_gram, left_basis, right_basis)
    left_fresh = refresh_basis(left_new, left_basis)
    right_fresh = refresh_basis(right_new, right_basis)
    keep_new = stale_flag > 0
    return (weight_new, moment_new, second_new, left_new, right_new, jnp.where(keep_new, left_fresh, left_basis), jnp.where(keep_new, right_fresh, right_basis))

def reference(activations, out_grads, weight, moment, second, left_gram, right_gram, left_basis, right_basis, slot_map, stale_mark):
    act_width = N_DP * BPD * B
    inputs = activations.reshape(N_DP, TOK_DEV, act_width).astype(jnp.float32)

    def column_grad(column):
        start_out = (column * B).astype(jnp.int32)
        outputs = lax.dynamic_slice_in_dim(out_grads, start_out, B, 1)
        outputs = outputs.reshape(N_DP, TOK_DEV, B).astype(jnp.float32)
        partial_sums = jnp.einsum('dtw,dtb->dwb', inputs, outputs, precision=highest)
        rounded = lax.optimization_barrier(partial_sums.astype(jnp.bfloat16))
        return lax.optimization_barrier(jnp.sum(rounded.astype(jnp.float32), axis=0))
    summed = lax.map(column_grad, jnp.arange(N_BLK, dtype=jnp.int32))
    grads = jnp.transpose(summed.reshape(N_BLK, N_DP, BPD, B, B), (1, 0, 2, 3, 4))
    picked_list = []
    for target in range(BPD):
        picked = grads[:, :, 0]
        for source in range(1, BPD):
            picked = jnp.where((slot_map[:, :, target] == source)[:, :, None, None], grads[:, :, source], picked)
        picked_list.append(picked)
    gradient = jnp.stack(picked_list, axis=2)
    total = N_DP * N_BLK * BPD

    def flatten(array):
        return array.reshape((total,) + array.shape[3:])
    results = lax.map(block_step, (flatten(gradient), flatten(weight), flatten(moment), flatten(second), flatten(left_gram), flatten(right_gram), flatten(left_basis), flatten(right_basis), flatten(stale_mark)))
    shaped = tuple((item.reshape(N_DP, N_BLK, BPD, B, B) for item in results))
    return (shaped[0], shaped[1], shaped[2], shaped[3], shaped[4], shaped[5], shaped[6])
```

```python
import jax
import jax.numpy as jnp
from jax import lax
from jax.experimental import pallas as pl
from jax.experimental.pallas import tpu as pltpu
from jax.sharding import PartitionSpec as P

highest = lax.Precision.HIGHEST
beta_one = 0.9
beta_two = 0.95
gram_beta = 0.95
eps_adam = 1e-08
learn_rate = 0.1
decay_rate = 0.01
bias_one = 1.0 - 0.9**10
bias_two = 1.0 - 0.95**10

NB = 32
GROUP = 8
f32 = jnp.float32
bf16 = jnp.bfloat16


def dot(a, b, ca=1, cb=0, precision=highest):
    return lax.dot_general(
        a, b, (((ca,), (cb,)), ((), ())), precision=precision, preferred_element_type=f32
    )


def split3(x):
    h = x.astype(bf16)
    r = x - h.astype(f32)
    m = r.astype(bf16)
    l = (r - m.astype(f32)).astype(bf16)
    return h, m, l


def inverse_factors(a):
    lane = lax.broadcasted_iota(jnp.int32, (NB, 128), 1)
    row = lax.broadcasted_iota(jnp.int32, (NB, 128), 0)
    e = jnp.where(lane % NB == row, 1.0, 0.0).astype(f32)
    pivots = []
    done_e = []
    for b in range(NB // GROUP):
        rows = NB - b * GROUP
        lane_b = lax.broadcasted_iota(jnp.int32, (rows, 128), 1)
        row_b = lax.broadcasted_iota(jnp.int32, (rows, 128), 0)
        base = lane_b - lane_b % NB
        v = [
            jnp.take_along_axis(a, base + (b * GROUP + j), axis=1)
            for j in range(GROUP)
        ]
        for k in range(GROUP):
            piv = v[k][k : k + 1, :]
            pivots.append(piv)
            rec = 1.0 / piv
            m = jnp.where(row_b > k, v[k] * rec, 0.0)
            for j in range(k + 1, GROUP):
                v[j] = v[j] - m * v[j][k : k + 1, :]
            a = a - m * a[k : k + 1, :]
            e = e - m * e[k : k + 1, :]
        done_e.append(e[:GROUP])
        a = a[GROUP:]
        e = e[GROUP:]
    scale = lax.rsqrt(jnp.concatenate(pivots, axis=0))
    return jnp.concatenate(done_e, axis=0) * scale


def refresh_all(w_ref, z_ref):
    panels = 256 // NB
    lane = lax.broadcasted_iota(jnp.int32, (NB, 128), 1)
    big_lane = lax.broadcasted_iota(jnp.int32, (128, 128), 1)
    big_row = lax.broadcasted_iota(jnp.int32, (128, 128), 0)
    for p in range(panels):
        tile = p // 4
        packed = None
        for t in range(4):
            x = w_ref[p, t * NB : (t + 1) * NB, tile * 128 : (tile + 1) * 128]
            shift = ((t - p % 4) * NB) % 128
            if shift:
                x = pltpu.roll(x, shift, 1)
            packed = x if packed is None else jnp.where(lane // NB == t, x, packed)
        inv = inverse_factors(packed)
        bd = jnp.where(
            big_lane // NB == big_row // NB, jnp.concatenate([inv] * 4, axis=0), 0.0
        )
        c0 = tile * 128
        r = dot(bd, w_ref[p, :, c0:])
        for t in range(4):
            rt = r[t * NB : (t + 1) * NB]
            z_ref[t, p * NB : (p + 1) * NB, :] = rt[:, 256 - c0 :]
        if p == panels - 1:
            break
        r0 = ((p + 1) // 4) * 128
        for t in range(4):
            h, m, l = split3(r[t * NB : (t + 1) * NB])
            lhs = jnp.concatenate([h, h, m, m, h, l], axis=0)[:, r0 - c0 : 256 - c0]
            rhs = jnp.concatenate([h, m, h, m, l, h], axis=0)[:, r0 - c0 :]
            u = dot(lhs, rhs, 0, 0, None)
            for q in range(p + 1, panels):
                at = q * NB - r0
                w_ref[q, t * NB : (t + 1) * NB, r0:] -= u[at : at + NB]


def state_kernel(
    slot_ref, stale_ref, g_ref, weight_ref, moment_ref, second_ref, lg_ref, rg_ref, lb_ref, rb_ref,
    weight_out, moment_out, second_out, left_out, right_out, lb_out, rb_out,
    w_ref, z_ref,
):
    def grams(i):
        g = g_ref[slot_ref[0, i]]
        coef = (1.0 - gram_beta) / 256
        left_out[i] = gram_beta * lg_ref[i] + coef * dot(g, g, 1, 1)
        right_out[i] = gram_beta * rg_ref[i] + coef * dot(g, g, 0, 0)

    def weights(i):
        g = g_ref[slot_ref[0, i]]
        left, right = lb_ref[i], rb_ref[i]
        moment_new = beta_one * moment_ref[i] + (1.0 - beta_one) * g
        moment_out[i] = moment_new
        rotated = dot(dot(left, g, 0, 0), right)
        second_new = beta_two * second_ref[i] + (1.0 - beta_two) * rotated * rotated
        second_out[i] = second_new
        turned = dot(dot(left, moment_new, 0, 0), right)
        normal = turned / bias_one / (jnp.sqrt(second_new / bias_two) + eps_adam)
        update = dot(dot(left, normal), right, 1, 1)
        wide = weight_ref[i].astype(f32)
        weight_out[i] = (wide - learn_rate * (update + decay_rate * wide)).astype(bf16)

    for i in range(2):
        grams(i)
    for i in range(2):
        weights(i)

    @pl.when(stale_ref[0, 0] > 0)
    def _():
        for i in range(2):
            for side, (s_ref, b_ref) in enumerate(((left_out, lb_ref), (right_out, rb_ref))):
                t = i * 2 + side
                z = dot(b_ref[i], s_ref[i], 0, 0)
                c = dot(z, z, 1, 1)
                for p in range(256 // NB):
                    w_ref[p, t * NB : (t + 1) * NB, :256] = c[p * NB : (p + 1) * NB]
                    w_ref[p, t * NB : (t + 1) * NB, 256:] = z[p * NB : (p + 1) * NB]
        refresh_all(w_ref, z_ref)
        for i in range(2):
            lb_out[i] = z_ref[i * 2].T
            rb_out[i] = z_ref[i * 2 + 1].T

    @pl.when(stale_ref[0, 0] <= 0)
    def _():
        lb_out[...] = lb_ref[...]
        rb_out[...] = rb_ref[...]


def state_step(g, weight, moment, second, lg, rg, lb, rb, slot, stale):
    block = jax.ShapeDtypeStruct((2, 256, 256), f32)
    vm = pl.BlockSpec(memory_space=pltpu.VMEM)
    sm = pl.BlockSpec(memory_space=pltpu.SMEM)
    return pl.pallas_call(
        state_kernel,
        out_shape=(jax.ShapeDtypeStruct((2, 256, 256), bf16),) + (block,) * 6,
        in_specs=[sm, sm] + [vm] * 8,
        out_specs=[vm] * 7,
        scratch_shapes=[pltpu.VMEM((8, 4 * NB, 512), f32), pltpu.VMEM((4, 256, 256), f32)],
        compiler_params=pltpu.CompilerParams(vmem_limit_bytes=48 * 1024 * 1024),
    )(slot, stale, g, weight, moment, second, lg, rg, lb, rb)


def local(
    activations, out_grads, weight, moment, second, left_gram, right_gram, left_basis, right_basis,
    slot_map, stale_mark,
):
    block_size = out_grads.shape[1]
    owned_count = weight.shape[2]
    features = lax.all_gather(activations, "blk", axis=1, tiled=True)
    summed = lax.psum_scatter(
        lax.dot_general(
            features, out_grads, (((0,), (0,)), ((), ())), preferred_element_type=f32
        ).astype(bf16),
        "dp",
        scatter_dimension=0,
        tiled=True,
    ).astype(f32)
    blocks = summed.reshape(owned_count, block_size, block_size)
    outs = state_step(
        blocks, weight[0, 0], moment[0, 0], second[0, 0], left_gram[0, 0], right_gram[0, 0],
        left_basis[0, 0], right_basis[0, 0], slot_map[0], stale_mark[0],
    )
    return tuple(item[None, None] for item in outs)


def solution(mesh):
    rows = P("dp", "blk")
    block = P("dp", "blk", None, None, None)
    marks = P("dp", "blk", None)
    return jax.shard_map(
        local,
        mesh=mesh,
        in_specs=(rows, rows) + (block,) * 7 + (marks, marks),
        out_specs=(block,) * 7,
        check_vma=False,
    )
```

```python
import jax
import jax.numpy as jnp
from jax import lax
from jax.experimental import pallas as pl
from jax.experimental.pallas import tpu as pltpu
from jax.sharding import PartitionSpec as P

f32 = jnp.float32
bf16 = jnp.bfloat16
MESH = pl.DeviceIdType.MESH


def gradient_kernel(
    a_ref, g_ref, out_ref, at_ref, gg_ref, part_ref, pair_send, pair_recv, sum_send, sum_recv,
    turn_send, a_sems, g_sems, pair_sems, sum_sems, turn_sems,
):
    dp, blk = lax.axis_index("dp"), lax.axis_index("blk")
    x, core = lax.div(dp, 2), lax.rem(dp, 2)
    y, z = lax.div(blk, 8), lax.rem(blk, 8)

    def device(x_to, core_to, y_to, z_to):
        return (x_to * 2 + core_to, y_to * 8 + z_to)

    z_right = device(x, core, y, lax.rem(z + 1, 8))
    z_left = device(x, core, y, lax.rem(z + 7, 8))
    y_up = device(x, core, lax.rem(y + 1, 4), z)
    y_down = device(x, core, lax.rem(y + 3, 4), z)
    other_core = device(x, 1 - core, y, z)
    x_far = [None] + [device(lax.rem(x + e, 4), core, y, z) for e in (1, 2, 3)]
    mirror = device(y, core, x, z)
    on_diagonal = x == y

    barrier = pltpu.get_barrier_semaphore()
    for partner in (z_right, z_left, y_up, y_down, other_core, *x_far[1:]):
        pl.semaphore_signal(barrier, inc=1, device_id=partner, device_id_type=MESH)

    @pl.when(jnp.logical_not(on_diagonal))
    def _():
        pl.semaphore_signal(barrier, inc=1, device_id=mirror, device_id_type=MESH)

    pl.semaphore_wait(barrier, jnp.where(on_diagonal, 8, 9))

    def remote(src, dst, sems, index, to):
        return pltpu.make_async_remote_copy(
            src_ref=src, dst_ref=dst, send_sem=sems.at[(0, *index)], recv_sem=sems.at[(1, *index)],
            device_id=to, device_id_type=MESH,
        )

    def g_copy(way, step, half):
        rows = pl.ds(half * 512, 512)
        src = g_ref.at[rows] if step == 0 else gg_ref.at[(1, 3)[way], rows]
        slot = ((1, 2), (3, 2))[way][step]
        return remote(src, gg_ref.at[slot, rows], g_sems, (way, step, half), (y_up, y_down)[way])

    def a_copy(way, step, half):
        rows = pl.ds(half * 64, 64)
        src_slot = step if way == 0 else (8 - step) % 8
        dst_slot = step + 1 if way == 0 else 7 - step
        return remote(
            at_ref.at[src_slot, rows], at_ref.at[dst_slot, rows], a_sems, (way, step, half),
            (z_right, z_left)[way],
        )

    def pass_on_a(step, half):
        for way in (0, 1):
            a_copy(way, step - 1, half).wait_recv()
            if step < 3 or half == way:
                a_copy(way, step, half).start()

    def product(s, low, high):
        lhs = at_ref[low:high].reshape((high - low) * 128, 1024)
        rhs = g_ref[...] if s == 0 else gg_ref[s]
        got = jnp.dot(lhs, rhs, preferred_element_type=f32)
        for r in range(low, high):
            part_ref[s, lax.rem(z + 8 - r, 8)] = got[(r - low) * 128 : (r - low + 1) * 128]

    for way in (0, 1):
        g_copy(way, 0, way).start()
    at_ref[0] = a_ref[...].T
    for half in (0, 1):
        for way in (0, 1):
            a_copy(way, 0, half).start()
    for way in (0, 1):
        g_copy(way, 0, 1 - way).start()
    product(0, 0, 1)
    pass_on_a(1, 0)
    for way in (0, 1):
        g_copy(way, 0, way).wait_recv()
        g_copy(way, 1, way).start()
    pass_on_a(1, 1)
    product(0, 1, 2)
    product(0, 7, 8)
    pass_on_a(2, 0)
    pass_on_a(2, 1)
    product(0, 2, 3)
    product(0, 6, 7)
    for way in (0, 1):
        g_copy(way, 0, 1 - way).wait_recv()
    product(1, 0, 3)
    product(1, 6, 8)
    product(3, 0, 3)
    pass_on_a(3, 0)
    product(3, 6, 8)
    pass_on_a(3, 1)
    product(0, 3, 4)
    product(0, 5, 6)
    product(1, 3, 4)
    product(1, 5, 6)
    product(3, 3, 4)
    product(3, 5, 6)
    for way in (0, 1):
        g_copy(way, 1, way).wait_recv()
    product(2, 0, 4)
    product(2, 5, 8)
    for way in (0, 1):
        a_copy(way, 3, way).wait_recv()
    for s in (0, 1, 3, 2):
        product(s, 4, 5)

    mine, theirs = core * 4, (1 - core) * 4

    def pair_copy(e):
        return remote(pair_send.at[e], pair_recv.at[e], pair_sems, (e,), other_core)

    def sum_copy(e):
        return remote(sum_send.at[e], sum_recv.at[e], sum_sems, (e,), x_far[e])

    def slot_for(e):
        return lax.rem(y + 8 - x - e, 4)

    order = (2, 1, 3, 0)
    for e in order:
        pair_send[e] = part_ref[slot_for(e), pl.ds(theirs, 4)].astype(bf16)
        pair_copy(e).start()
    for e in order[:3]:
        pair_copy(e).wait_recv()
        total = part_ref[slot_for(e), pl.ds(mine, 4)] + pair_recv[e].astype(f32)
        sum_send[e] = total.astype(bf16)
        sum_copy(e).start()
    pair_copy(0).wait_recv()
    total = part_ref[slot_for(0), pl.ds(mine, 4)] + pair_recv[0].astype(f32)
    for e in (1, 3, 2):
        sum_copy(e).wait_recv()
    total = total + sum_recv[1].astype(f32) + sum_recv[2].astype(f32) + sum_recv[3].astype(f32)
    turn_send[...] = total.astype(bf16)
    turn = remote(turn_send, out_ref, turn_sems, (), mirror)

    @pl.when(jnp.logical_not(on_diagonal))
    def _():
        turn.start()

    for way in (0, 1):
        for half in (0, 1):
            g_copy(way, 0, half).wait_send()
            for step in (0, 1, 2):
                a_copy(way, step, half).wait_send()
        g_copy(way, 1, way).wait_send()
        a_copy(way, 3, way).wait_send()
    for e in order:
        pair_copy(e).wait_send()
    for e in order[:3]:
        sum_copy(e).wait_send()

    @pl.when(on_diagonal)
    def _():
        out_ref[...] = turn_send[...]

    @pl.when(jnp.logical_not(on_diagonal))
    def _():
        turn.wait()


def gradient_sums(activations, out_grads):
    vm = pl.BlockSpec(memory_space=pltpu.VMEM)
    dma = pltpu.SemaphoreType.DMA
    piece = (4, 128, 256)
    return pl.pallas_call(
        gradient_kernel,
        out_shape=jax.ShapeDtypeStruct(piece, bf16),
        in_specs=[vm, vm],
        out_specs=vm,
        scratch_shapes=[
            pltpu.VMEM((8, 128, 1024), bf16),
            pltpu.VMEM((4, 1024, 256), bf16),
            pltpu.VMEM((4, 8, 128, 256), f32),
            pltpu.VMEM((4,) + piece, bf16),
            pltpu.VMEM((4,) + piece, bf16),
            pltpu.VMEM((4,) + piece, bf16),
            pltpu.VMEM((4,) + piece, bf16),
            pltpu.VMEM(piece, bf16),
            dma((2, 2, 4, 2)),
            dma((2, 2, 2, 2)),
            dma((2, 4)),
            dma((2, 4)),
            dma((2,)),
        ],
        compiler_params=pltpu.CompilerParams(
            collective_id=0, has_side_effects=True, vmem_limit_bytes=48 * 1024 * 1024
        ),
        cost_estimate=pl.CostEstimate(flops=2 * 1024**3, bytes_accessed=1 << 20, transcendentals=0),
    )(activations, out_grads)


highest = lax.Precision.HIGHEST
beta_one = 0.9
beta_two = 0.95
gram_beta = 0.95
eps_adam = 1e-08
learn_rate = 0.1
decay_rate = 0.01
bias_one = 1.0 - 0.9**10
bias_two = 1.0 - 0.95**10

NB = 32
GROUP = 8


def dot(a, b, ca=1, cb=0, precision=highest):
    return lax.dot_general(
        a, b, (((ca,), (cb,)), ((), ())), precision=precision, preferred_element_type=f32
    )


def split3(x):
    h = x.astype(bf16)
    r = x - h.astype(f32)
    m = r.astype(bf16)
    l = (r - m.astype(f32)).astype(bf16)
    return h, m, l


def inverse_factors(a):
    lane = lax.broadcasted_iota(jnp.int32, (NB, 128), 1)
    row = lax.broadcasted_iota(jnp.int32, (NB, 128), 0)
    e = jnp.where(lane % NB == row, 1.0, 0.0).astype(f32)
    pivots = []
    done_e = []
    for b in range(NB // GROUP):
        rows = NB - b * GROUP
        lane_b = lax.broadcasted_iota(jnp.int32, (rows, 128), 1)
        row_b = lax.broadcasted_iota(jnp.int32, (rows, 128), 0)
        base = lane_b - lane_b % NB
        v = [
            jnp.take_along_axis(a, base + (b * GROUP + j), axis=1)
            for j in range(GROUP)
        ]
        for k in range(GROUP):
            piv = v[k][k : k + 1, :]
            pivots.append(piv)
            rec = 1.0 / piv
            m = jnp.where(row_b > k, v[k] * rec, 0.0)
            for j in range(k + 1, GROUP):
                v[j] = v[j] - m * v[j][k : k + 1, :]
            a = a - m * a[k : k + 1, :]
            e = e - m * e[k : k + 1, :]
        done_e.append(e[:GROUP])
        a = a[GROUP:]
        e = e[GROUP:]
    scale = lax.rsqrt(jnp.concatenate(pivots, axis=0))
    return jnp.concatenate(done_e, axis=0) * scale


def refresh_all(w_ref, z_ref):
    panels = 256 // NB
    lane = lax.broadcasted_iota(jnp.int32, (NB, 128), 1)
    big_lane = lax.broadcasted_iota(jnp.int32, (128, 128), 1)
    big_row = lax.broadcasted_iota(jnp.int32, (128, 128), 0)
    for p in range(panels):
        tile = p // 4
        packed = None
        for t in range(4):
            x = w_ref[p, t * NB : (t + 1) * NB, tile * 128 : (tile + 1) * 128]
            shift = ((t - p % 4) * NB) % 128
            if shift:
                x = pltpu.roll(x, shift, 1)
            packed = x if packed is None else jnp.where(lane // NB == t, x, packed)
        inv = inverse_factors(packed)
        bd = jnp.where(
            big_lane // NB == big_row // NB, jnp.concatenate([inv] * 4, axis=0), 0.0
        )
        c0 = tile * 128
        r = dot(bd, w_ref[p, :, c0:])
        for t in range(4):
            rt = r[t * NB : (t + 1) * NB]
            z_ref[t, p * NB : (p + 1) * NB, :] = rt[:, 256 - c0 :]
        if p == panels - 1:
            break
        r0 = ((p + 1) // 4) * 128
        for t in range(4):
            h, m, l = split3(r[t * NB : (t + 1) * NB])
            lhs = jnp.concatenate([h, h, m, m, h, l], axis=0)[:, r0 - c0 : 256 - c0]
            rhs = jnp.concatenate([h, m, h, m, l, h], axis=0)[:, r0 - c0 :]
            u = dot(lhs, rhs, 0, 0, None)
            for q in range(p + 1, panels):
                at = q * NB - r0
                w_ref[q, t * NB : (t + 1) * NB, r0:] -= u[at : at + NB]


def state_kernel(
    slot_ref, stale_ref, g_ref, weight_ref, moment_ref, second_ref, lg_ref, rg_ref, lb_ref, rb_ref,
    weight_out, moment_out, second_out, left_out, right_out, lb_out, rb_out,
    w_ref, z_ref,
):
    def grams(i):
        g = g_ref[slot_ref[0, i]].astype(f32)
        coef = (1.0 - gram_beta) / 256
        left_out[i] = gram_beta * lg_ref[i] + coef * dot(g, g, 1, 1)
        right_out[i] = gram_beta * rg_ref[i] + coef * dot(g, g, 0, 0)

    def weights(i):
        g = g_ref[slot_ref[0, i]].astype(f32)
        left, right = lb_ref[i], rb_ref[i]
        moment_new = beta_one * moment_ref[i] + (1.0 - beta_one) * g
        moment_out[i] = moment_new
        rotated = dot(dot(left, g, 0, 0), right)
        second_new = beta_two * second_ref[i] + (1.0 - beta_two) * rotated * rotated
        second_out[i] = second_new
        turned = dot(dot(left, moment_new, 0, 0), right)
        normal = turned / bias_one / (jnp.sqrt(second_new / bias_two) + eps_adam)
        update = dot(dot(left, normal), right, 1, 1)
        wide = weight_ref[i].astype(f32)
        weight_out[i] = (wide - learn_rate * (update + decay_rate * wide)).astype(bf16)

    for i in range(2):
        grams(i)
    for i in range(2):
        weights(i)

    @pl.when(stale_ref[0, 0] > 0)
    def _():
        for i in range(2):
            for side, (s_ref, b_ref) in enumerate(((left_out, lb_ref), (right_out, rb_ref))):
                t = i * 2 + side
                z = dot(b_ref[i], s_ref[i], 0, 0)
                c = dot(z, z, 1, 1)
                for p in range(256 // NB):
                    w_ref[p, t * NB : (t + 1) * NB, :256] = c[p * NB : (p + 1) * NB]
                    w_ref[p, t * NB : (t + 1) * NB, 256:] = z[p * NB : (p + 1) * NB]
        refresh_all(w_ref, z_ref)
        for i in range(2):
            lb_out[i] = z_ref[i * 2].T
            rb_out[i] = z_ref[i * 2 + 1].T

    @pl.when(stale_ref[0, 0] <= 0)
    def _():
        lb_out[...] = lb_ref[...]
        rb_out[...] = rb_ref[...]


def state_step(g, weight, moment, second, lg, rg, lb, rb, slot, stale):
    block = jax.ShapeDtypeStruct((2, 256, 256), f32)
    vm = pl.BlockSpec(memory_space=pltpu.VMEM)
    sm = pl.BlockSpec(memory_space=pltpu.SMEM)
    return pl.pallas_call(
        state_kernel,
        out_shape=(jax.ShapeDtypeStruct((2, 256, 256), bf16),) + (block,) * 6,
        in_specs=[sm, sm] + [vm] * 8,
        out_specs=[vm] * 7,
        scratch_shapes=[pltpu.VMEM((8, 4 * NB, 512), f32), pltpu.VMEM((4, 256, 256), f32)],
        compiler_params=pltpu.CompilerParams(vmem_limit_bytes=48 * 1024 * 1024),
    )(slot, stale, g, weight, moment, second, lg, rg, lb, rb)


def local(
    activations, out_grads, weight, moment, second, left_gram, right_gram, left_basis, right_basis,
    slot_map, stale_mark,
):
    summed = gradient_sums(activations, out_grads)
    outs = state_step(
        summed.reshape(2, 256, 256), weight[0, 0], moment[0, 0], second[0, 0], left_gram[0, 0],
        right_gram[0, 0], left_basis[0, 0], right_basis[0, 0], slot_map[0], stale_mark[0],
    )
    return tuple(item[None, None] for item in outs)


def solution(mesh):
    rows = P("dp", "blk")
    block = P("dp", "blk", None, None, None)
    marks = P("dp", "blk", None)
    return jax.shard_map(
        local,
        mesh=mesh,
        in_specs=(rows, rows) + (block,) * 7 + (marks, marks),
        out_specs=(block,) * 7,
        check_vma=False,
    )
```

```python
import jax
import jax.numpy as jnp
from jax import lax
from jax.experimental import pallas as pl
from jax.experimental.pallas import tpu as pltpu
from jax.sharding import PartitionSpec as P

f32 = jnp.float32
bf16 = jnp.bfloat16
MESH = pl.DeviceIdType.MESH


def gradient_kernel(
    slot_hbm, a_ref, g_ref, out_ref, slot_ref, a_own, at_ref, gg_ref, part_ref, pair_send, pair_recv,
    y_send, y_recv, x_recv, total_ref, local_sems, a_sems, g_sems, pair_sems, y_sems, x_sems,
):
    loads = [
        pltpu.make_async_copy(src, dst, local_sems.at[i])
        for i, (src, dst) in enumerate(
            ((a_ref, a_own), (g_ref, gg_ref.at[0]), (slot_hbm, slot_ref))
        )
    ]
    for load in loads:
        load.start()
    dp, blk = lax.axis_index("dp"), lax.axis_index("blk")
    x, core = lax.div(dp, 2), lax.rem(dp, 2)
    y, z = lax.div(blk, 8), lax.rem(blk, 8)

    def device(x_to, core_to, y_to, z_to):
        return (x_to * 2 + core_to, y_to * 8 + z_to)

    z_right = device(x, core, y, lax.rem(z + 1, 8))
    z_left = device(x, core, y, lax.rem(z + 7, 8))
    y_far = [None] + [device(x, core, lax.rem(y + 4 - s, 4), z) for s in (1, 2, 3)]
    x_far = [None] + [device(lax.rem(x + e, 4), core, y, z) for e in (1, 2, 3)]
    y_up, y_down = y_far[3], y_far[1]
    other_core = device(x, 1 - core, y, z)

    barrier = pltpu.get_barrier_semaphore()
    for partner in (z_right, z_left, other_core, *y_far[1:], *x_far[1:]):
        pl.semaphore_signal(barrier, inc=1, device_id=partner, device_id_type=MESH)
    pl.semaphore_wait(barrier, 9)

    def remote(src, dst, sems, index, to):
        return pltpu.make_async_remote_copy(
            src_ref=src, dst_ref=dst, send_sem=sems.at[(0, *index)], recv_sem=sems.at[(1, *index)],
            device_id=to, device_id_type=MESH,
        )

    def g_copy(way, step, half):
        rows = pl.ds(half * 512, 512)
        src = g_ref.at[rows] if step == 0 else gg_ref.at[(1, 3)[way], rows]
        slot = ((1, 2), (3, 2))[way][step]
        return remote(src, gg_ref.at[slot, rows], g_sems, (way, step, half), (y_up, y_down)[way])

    def a_copy(way, step, half):
        rows = pl.ds(half * 64, 64)
        src_slot = step if way == 0 else (8 - step) % 8
        dst_slot = step + 1 if way == 0 else 7 - step
        return remote(
            at_ref.at[src_slot, rows], at_ref.at[dst_slot, rows], a_sems, (way, step, half),
            (z_right, z_left)[way],
        )

    def pass_on_a(step, half):
        for way in (0, 1):
            a_copy(way, step - 1, half).wait_recv()
            if step < 3 or half == way:
                a_copy(way, step, half).start()

    def product(s, low, high):
        lhs = at_ref[low:high].reshape((high - low) * 128, 1024)
        got = jnp.dot(lhs, gg_ref[s], preferred_element_type=f32)
        for r in range(low, high):
            part_ref[s, lax.rem(z + 8 - r, 8)] = got[(r - low) * 128 : (r - low + 1) * 128]

    for way in (0, 1):
        g_copy(way, 0, way).start()
    loads[0].wait()
    at_ref[0] = a_own[...].T
    for half in (0, 1):
        for way in (0, 1):
            a_copy(way, 0, half).start()
    for way in (0, 1):
        g_copy(way, 0, 1 - way).start()
    loads[1].wait()
    product(0, 0, 1)
    pass_on_a(1, 0)
    for way in (0, 1):
        g_copy(way, 0, way).wait_recv()
        g_copy(way, 1, way).start()
    pass_on_a(1, 1)
    product(0, 1, 2)
    product(0, 7, 8)
    pass_on_a(2, 0)
    pass_on_a(2, 1)
    product(0, 2, 3)
    product(0, 6, 7)
    for way in (0, 1):
        g_copy(way, 0, 1 - way).wait_recv()
    product(1, 0, 3)
    product(1, 6, 8)
    product(3, 0, 3)
    pass_on_a(3, 0)
    product(3, 6, 8)
    def pair_copy(u):
        return remote(pair_send.at[u], pair_recv.at[u], pair_sems, (u,), other_core)

    def y_copy(u, s):
        return remote(y_send.at[u, s], y_recv.at[u, s], y_sems, (u, s), y_far[s])

    def x_slot(e):
        return lax.rem(x + 4 + e - y, 4)

    def x_copy(u, e):
        return remote(y_recv.at[u, x_slot(e)], x_recv.at[u, e], x_sems, (u, e), x_far[e])

    def chunk(u, whose):
        return whose * 4 + lax.rem(z + 8 - u, 4)

    def share(u):
        pair_send[u] = part_ref[:, chunk(u, 1 - core)].astype(bf16)
        pair_copy(u).start()

    def spread(u):
        pair_copy(u).wait_recv()
        for s in (2, 1, 3):
            y_send[u, s] = (part_ref[s, chunk(u, core)] + pair_recv[u, s].astype(f32)).astype(bf16)
            y_copy(u, s).start()
        y_recv[u, 0] = (part_ref[0, chunk(u, core)] + pair_recv[u, 0].astype(f32)).astype(bf16)

    def cross(u):
        for s in (1, 2, 3):
            y_copy(u, s).wait_recv()
        for e in (2, 1, 3):
            x_copy(u, e).start()

    def finish(u):
        total = y_recv[u, x_slot(0)].astype(f32)
        for e in (1, 2, 3):
            x_copy(u, e).wait_recv()
            total = total + x_recv[u, e].astype(f32)
        total_ref[lax.rem(z + 8 - u, 4)] = total

    for way in (0, 1):
        g_copy(way, 1, way).wait_recv()
    product(2, 2, 3)
    product(2, 6, 7)
    share(2)
    pass_on_a(3, 1)
    for s in (0, 1, 3):
        product(s, 3, 4)
        product(s, 5, 6)
    product(2, 1, 2)
    product(2, 5, 6)
    share(1)
    product(2, 3, 4)
    product(2, 7, 8)
    share(3)
    product(2, 0, 1)
    spread(2)
    spread(1)
    spread(3)
    cross(2)
    for way in (0, 1):
        a_copy(way, 3, way).wait_recv()
    for s in (0, 1, 3, 2):
        product(s, 4, 5)
    share(0)
    cross(1)
    spread(0)
    cross(3)
    finish(2)
    finish(1)
    cross(0)
    finish(3)
    finish(0)

    for way in (0, 1):
        for half in (0, 1):
            g_copy(way, 0, half).wait_send()
            for step in (0, 1, 2):
                a_copy(way, step, half).wait_send()
        g_copy(way, 1, way).wait_send()
        a_copy(way, 3, way).wait_send()
    for u in range(4):
        pair_copy(u).wait_send()
        for e in (1, 2, 3):
            y_copy(u, e).wait_send()
            x_copy(u, e).wait_send()
    loads[2].wait()
    for j in (0, 1):
        out_ref[j] = total_ref[pl.ds(slot_ref[0, j] * 2, 2)].reshape(256, 256)


def gradient_sums(slot_map, activations, out_grads):
    vm = pl.BlockSpec(memory_space=pltpu.VMEM)
    hbm = pl.BlockSpec(memory_space=pltpu.HBM)
    dma = pltpu.SemaphoreType.DMA
    return pl.pallas_call(
        gradient_kernel,
        out_shape=jax.ShapeDtypeStruct((2, 256, 256), f32),
        in_specs=[hbm] * 3,
        out_specs=vm,
        scratch_shapes=[
            pltpu.SMEM((1, 2), jnp.int32),
            pltpu.VMEM((1024, 128), bf16),
            pltpu.VMEM((8, 128, 1024), bf16),
            pltpu.VMEM((4, 1024, 256), bf16),
            pltpu.VMEM((4, 8, 128, 256), f32),
            pltpu.VMEM((4, 4, 128, 256), bf16),
            pltpu.VMEM((4, 4, 128, 256), bf16),
            pltpu.VMEM((4, 4, 128, 256), bf16),
            pltpu.VMEM((4, 4, 128, 256), bf16),
            pltpu.VMEM((4, 4, 128, 256), bf16),
            pltpu.VMEM((4, 128, 256), f32),
            dma((3,)),
            dma((2, 2, 4, 2)),
            dma((2, 2, 2, 2)),
            dma((2, 4)),
            dma((2, 4, 4)),
            dma((2, 4, 4)),
        ],
        compiler_params=pltpu.CompilerParams(
            collective_id=0, has_side_effects=True, vmem_limit_bytes=40 * 1024 * 1024
        ),
        cost_estimate=pl.CostEstimate(flops=2 * 1024**3, bytes_accessed=1 << 20, transcendentals=0),
    )(slot_map, activations, out_grads)


highest = lax.Precision.HIGHEST
beta_one = 0.9
beta_two = 0.95
gram_beta = 0.95
eps_adam = 1e-08
learn_rate = 0.1
decay_rate = 0.01
bias_one = 1.0 - 0.9**10
bias_two = 1.0 - 0.95**10

NB = 32
GROUP = 8


def dot(a, b, ca=1, cb=0, precision=highest):
    return lax.dot_general(
        a, b, (((ca,), (cb,)), ((), ())), precision=precision, preferred_element_type=f32
    )


def split3(x):
    h = x.astype(bf16)
    r = x - h.astype(f32)
    m = r.astype(bf16)
    l = (r - m.astype(f32)).astype(bf16)
    return h, m, l


def inverse_factors(a):
    lane = lax.broadcasted_iota(jnp.int32, (NB, 128), 1)
    row = lax.broadcasted_iota(jnp.int32, (NB, 128), 0)
    e = jnp.where(lane % NB == row, 1.0, 0.0).astype(f32)
    pivots = []
    done_e = []
    for b in range(NB // GROUP):
        rows = NB - b * GROUP
        lane_b = lax.broadcasted_iota(jnp.int32, (rows, 128), 1)
        row_b = lax.broadcasted_iota(jnp.int32, (rows, 128), 0)
        base = lane_b - lane_b % NB
        v = [
            jnp.take_along_axis(a, base + (b * GROUP + j), axis=1)
            for j in range(GROUP)
        ]
        for k in range(GROUP):
            piv = v[k][k : k + 1, :]
            pivots.append(piv)
            rec = 1.0 / piv
            m = jnp.where(row_b > k, v[k] * rec, 0.0)
            for j in range(k + 1, GROUP):
                v[j] = v[j] - m * v[j][k : k + 1, :]
            a = a - m * a[k : k + 1, :]
            e = e - m * e[k : k + 1, :]
        done_e.append(e[:GROUP])
        a = a[GROUP:]
        e = e[GROUP:]
    scale = lax.rsqrt(jnp.concatenate(pivots, axis=0))
    return jnp.concatenate(done_e, axis=0) * scale


def refresh_all(w_ref, z_ref):
    panels = 256 // NB
    lane = lax.broadcasted_iota(jnp.int32, (NB, 128), 1)
    big_lane = lax.broadcasted_iota(jnp.int32, (128, 128), 1)
    big_row = lax.broadcasted_iota(jnp.int32, (128, 128), 0)
    for p in range(panels):
        tile = p // 4
        packed = None
        for t in range(4):
            x = w_ref[p, t * NB : (t + 1) * NB, tile * 128 : (tile + 1) * 128]
            shift = ((t - p % 4) * NB) % 128
            if shift:
                x = pltpu.roll(x, shift, 1)
            packed = x if packed is None else jnp.where(lane // NB == t, x, packed)
        inv = inverse_factors(packed)
        bd = jnp.where(
            big_lane // NB == big_row // NB, jnp.concatenate([inv] * 4, axis=0), 0.0
        )
        c0 = tile * 128
        r = dot(bd, w_ref[p, :, c0:])
        for t in range(4):
            rt = r[t * NB : (t + 1) * NB]
            z_ref[t, p * NB : (p + 1) * NB, :] = rt[:, 256 - c0 :]
        if p == panels - 1:
            break
        r0 = ((p + 1) // 4) * 128
        for t in range(4):
            h, m, l = split3(r[t * NB : (t + 1) * NB])
            lhs = jnp.concatenate([h, h, m, m, h, l], axis=0)[:, r0 - c0 : 256 - c0]
            rhs = jnp.concatenate([h, m, h, m, l, h], axis=0)[:, r0 - c0 :]
            u = dot(lhs, rhs, 0, 0, None)
            for q in range(p + 1, panels):
                at = q * NB - r0
                w_ref[q, t * NB : (t + 1) * NB, r0:] -= u[at : at + NB]


def state_kernel(
    stale_ref, g_ref, weight_ref, moment_ref, second_ref, lg_ref, rg_ref, lb_ref, rb_ref,
    weight_out, moment_out, second_out, left_out, right_out, lb_out, rb_out,
    w_ref, z_ref,
):
    def grams(i):
        g = g_ref[i]
        coef = (1.0 - gram_beta) / 256
        left_out[i] = gram_beta * lg_ref[i] + coef * dot(g, g, 1, 1)
        right_out[i] = gram_beta * rg_ref[i] + coef * dot(g, g, 0, 0)

    def weights(i):
        g = g_ref[i]
        left, right = lb_ref[i], rb_ref[i]
        moment_new = beta_one * moment_ref[i] + (1.0 - beta_one) * g
        moment_out[i] = moment_new
        rotated = dot(dot(left, g, 0, 0), right)
        second_new = beta_two * second_ref[i] + (1.0 - beta_two) * rotated * rotated
        second_out[i] = second_new
        turned = dot(dot(left, moment_new, 0, 0), right)
        normal = turned / bias_one / (jnp.sqrt(second_new / bias_two) + eps_adam)
        update = dot(dot(left, normal), right, 1, 1)
        wide = weight_ref[i].astype(f32)
        weight_out[i] = (wide - learn_rate * (update + decay_rate * wide)).astype(bf16)

    for i in range(2):
        grams(i)
    for i in range(2):
        weights(i)

    @pl.when(stale_ref[0, 0] > 0)
    def _():
        for i in range(2):
            for side, (s_ref, b_ref) in enumerate(((left_out, lb_ref), (right_out, rb_ref))):
                t = i * 2 + side
                z = dot(b_ref[i], s_ref[i], 0, 0)
                c = dot(z, z, 1, 1)
                for p in range(256 // NB):
                    w_ref[p, t * NB : (t + 1) * NB, :256] = c[p * NB : (p + 1) * NB]
                    w_ref[p, t * NB : (t + 1) * NB, 256:] = z[p * NB : (p + 1) * NB]
        refresh_all(w_ref, z_ref)
        for i in range(2):
            lb_out[i] = z_ref[i * 2].T
            rb_out[i] = z_ref[i * 2 + 1].T

    @pl.when(stale_ref[0, 0] <= 0)
    def _():
        lb_out[...] = lb_ref[...]
        rb_out[...] = rb_ref[...]


def state_step(g, weight, moment, second, lg, rg, lb, rb, stale):
    block = jax.ShapeDtypeStruct((2, 256, 256), f32)
    vm = pl.BlockSpec(memory_space=pltpu.VMEM)
    sm = pl.BlockSpec(memory_space=pltpu.SMEM)
    return pl.pallas_call(
        state_kernel,
        out_shape=(jax.ShapeDtypeStruct((2, 256, 256), bf16),) + (block,) * 6,
        in_specs=[sm] + [vm] * 8,
        out_specs=[vm] * 7,
        scratch_shapes=[pltpu.VMEM((8, 4 * NB, 512), f32), pltpu.VMEM((4, 256, 256), f32)],
        compiler_params=pltpu.CompilerParams(vmem_limit_bytes=48 * 1024 * 1024),
    )(stale, g, weight, moment, second, lg, rg, lb, rb)


def local(
    activations, out_grads, weight, moment, second, left_gram, right_gram, left_basis, right_basis,
    slot_map, stale_mark,
):
    gradient = gradient_sums(slot_map[0], activations, out_grads)
    outs = state_step(
        gradient, weight[0, 0], moment[0, 0], second[0, 0], left_gram[0, 0],
        right_gram[0, 0], left_basis[0, 0], right_basis[0, 0], stale_mark[0],
    )
    return tuple(item[None, None] for item in outs)


def solution(mesh):
    rows = P("dp", "blk")
    block = P("dp", "blk", None, None, None)
    marks = P("dp", "blk", None)
    return jax.shard_map(
        local,
        mesh=mesh,
        in_specs=(rows, rows) + (block,) * 7 + (marks, marks),
        out_specs=(block,) * 7,
        check_vma=False,
    )
```

```python
import jax
import jax.numpy as jnp
from jax import lax
from jax.experimental import pallas as pl
from jax.experimental.pallas import tpu as pltpu
from jax.sharding import PartitionSpec as P

f32 = jnp.float32
bf16 = jnp.bfloat16
MESH = pl.DeviceIdType.MESH


def gradient_kernel(
    slot_hbm, a_ref, g_ref, out_ref, slot_ref, a_own, at_ref, gg_ref, part_ref, pair_send, pair_recv,
    y_send, y_recv, x_recv, total_ref, local_sems, a_sems, g_sems, pair_sems, y_sems, x_sems,
):
    loads = [
        pltpu.make_async_copy(src, dst, local_sems.at[i])
        for i, (src, dst) in enumerate(
            ((a_ref, a_own), (g_ref, gg_ref.at[0]), (slot_hbm, slot_ref))
        )
    ]
    for load in loads:
        load.start()
    dp, blk = lax.axis_index("dp"), lax.axis_index("blk")
    x, core = lax.div(dp, 2), lax.rem(dp, 2)
    y, z = lax.div(blk, 8), lax.rem(blk, 8)

    def device(x_to, core_to, y_to, z_to):
        return (x_to * 2 + core_to, y_to * 8 + z_to)

    z_right = device(x, core, y, lax.rem(z + 1, 8))
    z_left = device(x, core, y, lax.rem(z + 7, 8))
    y_far = [None] + [device(x, core, lax.rem(y + 4 - s, 4), z) for s in (1, 2, 3)]
    x_far = [None] + [device(lax.rem(x + e, 4), core, y, z) for e in (1, 2, 3)]
    y_up, y_down = y_far[3], y_far[1]
    other_core = device(x, 1 - core, y, z)

    barrier = pltpu.get_barrier_semaphore()
    for partner in (z_right, z_left, other_core, *y_far[1:], *x_far[1:]):
        pl.semaphore_signal(barrier, inc=1, device_id=partner, device_id_type=MESH)
    pl.semaphore_wait(barrier, 9)

    def remote(src, dst, sems, index, to):
        return pltpu.make_async_remote_copy(
            src_ref=src, dst_ref=dst, send_sem=sems.at[(0, *index)], recv_sem=sems.at[(1, *index)],
            device_id=to, device_id_type=MESH,
        )

    def g_copy(way, step, half):
        rows = pl.ds(half * 512, 512)
        src = g_ref.at[rows] if step == 0 else gg_ref.at[(1, 3)[way], rows]
        slot = ((1, 2), (3, 2))[way][step]
        return remote(src, gg_ref.at[slot, rows], g_sems, (way, step, half), (y_up, y_down)[way])

    def a_copy(way, step, half):
        rows = pl.ds(half * 64, 64)
        src_slot = step if way == 0 else (8 - step) % 8
        dst_slot = step + 1 if way == 0 else 7 - step
        return remote(
            at_ref.at[src_slot, rows], at_ref.at[dst_slot, rows], a_sems, (way, step, half),
            (z_right, z_left)[way],
        )

    def pass_on_a(step, half):
        for way in (0, 1):
            a_copy(way, step - 1, half).wait_recv()
            if step < 3 or half == way:
                a_copy(way, step, half).start()

    def product(s, low, high):
        lhs = at_ref[low:high].reshape((high - low) * 128, 1024)
        got = jnp.dot(lhs, gg_ref[s], preferred_element_type=f32)
        for r in range(low, high):
            part_ref[s, lax.rem(z + 8 - r, 8)] = got[(r - low) * 128 : (r - low + 1) * 128]

    for way in (0, 1):
        g_copy(way, 0, way).start()
    loads[0].wait()
    at_ref[0] = a_own[...].T
    for half in (0, 1):
        for way in (0, 1):
            a_copy(way, 0, half).start()
    for way in (0, 1):
        g_copy(way, 0, 1 - way).start()
    loads[1].wait()
    product(0, 0, 1)
    pass_on_a(1, 0)
    for way in (0, 1):
        g_copy(way, 0, way).wait_recv()
        g_copy(way, 1, way).start()
    pass_on_a(1, 1)
    product(0, 1, 2)
    product(0, 7, 8)
    pass_on_a(2, 0)
    pass_on_a(2, 1)
    product(0, 2, 3)
    product(0, 6, 7)
    for way in (0, 1):
        g_copy(way, 0, 1 - way).wait_recv()
    product(1, 0, 3)
    product(1, 6, 8)
    product(3, 0, 3)
    pass_on_a(3, 0)
    product(3, 6, 8)
    def pair_copy(u):
        return remote(pair_send.at[u], pair_recv.at[u], pair_sems, (u,), other_core)

    def y_copy(u, s):
        return remote(y_send.at[u, s], y_recv.at[u, s], y_sems, (u, s), y_far[s])

    def x_slot(e):
        return lax.rem(x + 4 + e - y, 4)

    def x_copy(u, e):
        return remote(y_recv.at[u, x_slot(e)], x_recv.at[u, e], x_sems, (u, e), x_far[e])

    def chunk(u, whose):
        return whose * 4 + lax.rem(z + 8 - u, 4)

    def share(u):
        pair_send[u] = part_ref[:, chunk(u, 1 - core)].astype(bf16)
        pair_copy(u).start()

    def spread(u):
        pair_copy(u).wait_recv()
        for s in (2, 1, 3):
            y_send[u, s] = (part_ref[s, chunk(u, core)] + pair_recv[u, s].astype(f32)).astype(bf16)
            y_copy(u, s).start()
        y_recv[u, 0] = (part_ref[0, chunk(u, core)] + pair_recv[u, 0].astype(f32)).astype(bf16)

    def cross(u):
        for s in (1, 2, 3):
            y_copy(u, s).wait_recv()
        for e in (2, 1, 3):
            x_copy(u, e).start()

    def finish(u):
        total = y_recv[u, x_slot(0)].astype(f32)
        for e in (1, 2, 3):
            x_copy(u, e).wait_recv()
            total = total + x_recv[u, e].astype(f32)
        total_ref[lax.rem(z + 8 - u, 4)] = total

    for way in (0, 1):
        g_copy(way, 1, way).wait_recv()
    product(2, 2, 3)
    product(2, 6, 7)
    share(2)
    pass_on_a(3, 1)
    for s in (0, 1, 3):
        product(s, 3, 4)
        product(s, 5, 6)
    product(2, 1, 2)
    product(2, 5, 6)
    share(1)
    product(2, 3, 4)
    product(2, 7, 8)
    share(3)
    product(2, 0, 1)
    spread(2)
    spread(1)
    spread(3)
    cross(2)
    for way in (0, 1):
        a_copy(way, 3, way).wait_recv()
    for s in (0, 1, 3, 2):
        product(s, 4, 5)
    share(0)
    cross(1)
    spread(0)
    cross(3)
    finish(2)
    finish(1)
    cross(0)
    finish(3)
    finish(0)

    for way in (0, 1):
        for half in (0, 1):
            g_copy(way, 0, half).wait_send()
            for step in (0, 1, 2):
                a_copy(way, step, half).wait_send()
        g_copy(way, 1, way).wait_send()
        a_copy(way, 3, way).wait_send()
    for u in range(4):
        pair_copy(u).wait_send()
        for e in (1, 2, 3):
            y_copy(u, e).wait_send()
            x_copy(u, e).wait_send()
    loads[2].wait()
    for j in (0, 1):
        out_ref[j] = total_ref[pl.ds(slot_ref[0, j] * 2, 2)].reshape(256, 256)


def gradient_sums(slot_map, activations, out_grads):
    vm = pl.BlockSpec(memory_space=pltpu.VMEM)
    hbm = pl.BlockSpec(memory_space=pltpu.HBM)
    dma = pltpu.SemaphoreType.DMA
    return pl.pallas_call(
        gradient_kernel,
        out_shape=jax.ShapeDtypeStruct((2, 256, 256), f32),
        in_specs=[hbm] * 3,
        out_specs=vm,
        scratch_shapes=[
            pltpu.SMEM((1, 2), jnp.int32),
            pltpu.VMEM((1024, 128), bf16),
            pltpu.VMEM((8, 128, 1024), bf16),
            pltpu.VMEM((4, 1024, 256), bf16),
            pltpu.VMEM((4, 8, 128, 256), f32),
            pltpu.VMEM((4, 4, 128, 256), bf16),
            pltpu.VMEM((4, 4, 128, 256), bf16),
            pltpu.VMEM((4, 4, 128, 256), bf16),
            pltpu.VMEM((4, 4, 128, 256), bf16),
            pltpu.VMEM((4, 4, 128, 256), bf16),
            pltpu.VMEM((4, 128, 256), f32),
            dma((3,)),
            dma((2, 2, 4, 2)),
            dma((2, 2, 2, 2)),
            dma((2, 4)),
            dma((2, 4, 4)),
            dma((2, 4, 4)),
        ],
        compiler_params=pltpu.CompilerParams(
            collective_id=0, has_side_effects=True, vmem_limit_bytes=40 * 1024 * 1024
        ),
        cost_estimate=pl.CostEstimate(flops=2 * 1024**3, bytes_accessed=1 << 20, transcendentals=0),
    )(*[pltpu.with_memory_space_constraint(item, pltpu.HBM) for item in (slot_map, activations, out_grads)])


highest = lax.Precision.HIGHEST
beta_one = 0.9
beta_two = 0.95
gram_beta = 0.95
eps_adam = 1e-08
learn_rate = 0.1
decay_rate = 0.01
bias_one = 1.0 - 0.9**10
bias_two = 1.0 - 0.95**10

NB = 32
GROUP = 8


def dot(a, b, ca=1, cb=0, precision=highest):
    return lax.dot_general(
        a, b, (((ca,), (cb,)), ((), ())), precision=precision, preferred_element_type=f32
    )


def split2(x):
    h = x.astype(bf16)
    return h, (x - h.astype(f32)).astype(bf16)


def dot3(a, b, ca=1, cb=0):
    return dot(
        jnp.concatenate([a[0], a[0], a[1]], axis=ca),
        jnp.concatenate([b[0], b[1], b[0]], axis=cb),
        ca, cb, None,
    )


def split3(x):
    h = x.astype(bf16)
    r = x - h.astype(f32)
    m = r.astype(bf16)
    l = (r - m.astype(f32)).astype(bf16)
    return h, m, l


def inverse_factors(a):
    lane = lax.broadcasted_iota(jnp.int32, (NB, 128), 1)
    row = lax.broadcasted_iota(jnp.int32, (NB, 128), 0)
    e = jnp.where(lane % NB == row, 1.0, 0.0).astype(f32)
    pivots = []
    done_e = []
    for b in range(NB // GROUP):
        rows = NB - b * GROUP
        lane_b = lax.broadcasted_iota(jnp.int32, (rows, 128), 1)
        row_b = lax.broadcasted_iota(jnp.int32, (rows, 128), 0)
        base = lane_b - lane_b % NB
        v = [
            jnp.take_along_axis(a, base + (b * GROUP + j), axis=1)
            for j in range(GROUP)
        ]
        for k in range(GROUP):
            piv = v[k][k : k + 1, :]
            pivots.append(piv)
            rec = 1.0 / piv
            m = jnp.where(row_b > k, v[k] * rec, 0.0)
            for j in range(k + 1, GROUP):
                v[j] = v[j] - m * v[j][k : k + 1, :]
            a = a - m * a[k : k + 1, :]
            e = e - m * e[k : k + 1, :]
        done_e.append(e[:GROUP])
        a = a[GROUP:]
        e = e[GROUP:]
    scale = lax.rsqrt(jnp.concatenate(pivots, axis=0))
    return jnp.concatenate(done_e, axis=0) * scale


def stacked_dot(lhs, rhs, ca, cb):
    h, m, l = split3(lhs)
    first = jnp.concatenate([h, h, m, m, h, l], axis=ca)
    h, m, l = split3(rhs)
    return dot(first, jnp.concatenate([h, m, h, m, l, h], axis=cb), ca, cb, None)


def refresh_all(w_ref, z_ref, beside):
    lane = lax.broadcasted_iota(jnp.int32, (NB, 128), 1)
    big_lane = lax.broadcasted_iota(jnp.int32, (128, 128), 1)
    big_row = lax.broadcasted_iota(jnp.int32, (128, 128), 0)
    for tile in range(2):
        c0 = tile * 128
        held = []
        for i in range(4):
            p = tile * 4 + i
            beside[p]()
            packed = None
            for t in range(4):
                x = w_ref[p, t * NB : (t + 1) * NB, c0 : c0 + 128]
                shift = ((t - i) * NB) % 128
                if shift:
                    x = pltpu.roll(x, shift, 1)
                packed = x if packed is None else jnp.where(lane // NB == t, x, packed)
            inv = inverse_factors(packed)
            bd = jnp.where(
                big_lane // NB == big_row // NB, jnp.concatenate([inv] * 4, axis=0), 0.0
            )
            r = stacked_dot(bd, w_ref[p, :, c0:], 1, 0)
            held.append(r)
            for t in range(4):
                z_ref[t, p * NB : (p + 1) * NB, :] = r[t * NB : (t + 1) * NB, 256 - c0 :]
            if i == 3:
                break
            for t in range(4):
                h, m, l = split3(r[t * NB : (t + 1) * NB])
                lhs = jnp.concatenate([h, h, m, m, h, l], axis=0)[:, :128].T[(i + 1) * NB :]
                rhs = jnp.concatenate([h, m, h, m, l, h], axis=0)
                u = dot(lhs, rhs, 1, 0, None)
                for q in range(i + 1, 4):
                    at = (q - i - 1) * NB
                    w_ref[tile * 4 + q, t * NB : (t + 1) * NB, c0:] -= u[at : at + NB]
        if tile == 0:
            for t in range(4):
                rows = jnp.concatenate([r[t * NB : (t + 1) * NB, 128:] for r in held], axis=0)
                u = stacked_dot(rows[:, :128], rows, 0, 0)
                for q in range(4):
                    w_ref[4 + q, t * NB : (t + 1) * NB, 128:] -= u[q * NB : (q + 1) * NB]


def state_kernel(
    stale_ref, g_ref, weight_ref, moment_ref, second_ref, lg_ref, rg_ref, lb_ref, rb_ref,
    weight_hbm, moment_hbm, second_hbm, left_hbm, right_hbm, lb_hbm, rb_hbm,
    weight_out, moment_out, second_out, left_out, right_out, lb_out, rb_out, w_ref, z_ref, sems,
):
    results = (weight_hbm, moment_hbm, second_hbm, left_hbm, right_hbm, lb_hbm, rb_hbm)

    def store(k, i, src):
        return pltpu.make_async_copy(src.at[i], results[k].at[i], sems.at[k, i])

    coef = (1.0 - gram_beta) / 256
    for i in range(2):
        g = g_ref[i]
        rows, columns = split2(g), split2(g.T)
        left_out[i] = gram_beta * lg_ref[i] + coef * dot3(rows, rows, 1, 1)
        right_out[i] = gram_beta * rg_ref[i] + coef * dot3(columns, columns, 1, 1)
        store(3, i, left_out).start()
        store(4, i, right_out).start()

    def weight_steps(i):
        held = {}

        def rotate_left():
            g = g_ref[i]
            moment_new = beta_one * moment_ref[i] + (1.0 - beta_one) * g
            moment_out[i] = moment_new
            store(1, i, moment_out).start()
            both = split2(jnp.concatenate([g, moment_new], axis=1))
            held["half"] = dot3(split2(lb_ref[i].T), both)

        def rotate_right():
            half = held.pop("half")
            both = split2(jnp.concatenate([half[:, :256], half[:, 256:]], axis=0))
            turned = dot3(both, split2(rb_ref[i]))
            rotated, turned = turned[:256], turned[256:]
            second_new = beta_two * second_ref[i] + (1.0 - beta_two) * rotated * rotated
            second_out[i] = second_new
            store(2, i, second_out).start()
            held["normal"] = turned / bias_one / (jnp.sqrt(second_new / bias_two) + eps_adam)

        def back_left():
            held["back"] = dot3(split2(lb_ref[i]), split2(held.pop("normal")))

        def back_right():
            update = dot3(split2(held.pop("back")), split2(rb_ref[i]), 1, 1)
            wide = weight_ref[i].astype(f32)
            weight_out[i] = (wide - learn_rate * (update + decay_rate * wide)).astype(bf16)
            store(0, i, weight_out).start()

        return [rotate_left, rotate_right, back_left, back_right]

    @pl.when(stale_ref[0, 0] > 0)
    def _():
        for i in range(2):
            for side, (s_ref, b_ref) in enumerate(((left_out, lb_ref), (right_out, rb_ref))):
                t = i * 2 + side
                z = dot3(split2(b_ref[i].T), split2(s_ref[i]))
                c = stacked_dot(z, z, 1, 1)
                for p in range(256 // NB):
                    w_ref[p, t * NB : (t + 1) * NB, :256] = c[p * NB : (p + 1) * NB]
                    w_ref[p, t * NB : (t + 1) * NB, 256:] = z[p * NB : (p + 1) * NB]
        refresh_all(w_ref, z_ref, weight_steps(0) + weight_steps(1))
        for i in range(2):
            lb_out[i] = z_ref[i * 2].T
            store(5, i, lb_out).start()
            rb_out[i] = z_ref[i * 2 + 1].T
            store(6, i, rb_out).start()

    @pl.when(stale_ref[0, 0] <= 0)
    def _():
        for i in range(2):
            store(5, i, lb_ref).start()
            store(6, i, rb_ref).start()
            for step in weight_steps(i):
                step()

    for k, src in enumerate((weight_out, moment_out, second_out, left_out, right_out, lb_out, rb_out)):
        for i in range(2):
            store(k, i, src).wait()


def state_step(g, weight, moment, second, lg, rg, lb, rb, stale):
    shape = (2, 256, 256)
    block = jax.ShapeDtypeStruct(shape, f32)
    vm = pl.BlockSpec(memory_space=pltpu.VMEM)
    sm = pl.BlockSpec(memory_space=pltpu.SMEM)
    return pl.pallas_call(
        state_kernel,
        out_shape=(jax.ShapeDtypeStruct(shape, bf16),) + (block,) * 6,
        in_specs=[sm] + [vm] * 8,
        out_specs=[pl.BlockSpec(memory_space=pltpu.HBM)] * 7,
        scratch_shapes=[pltpu.VMEM(shape, bf16)]
        + [pltpu.VMEM(shape, f32)] * 6
        + [
            pltpu.VMEM((8, 4 * NB, 512), f32),
            pltpu.VMEM((4, 256, 256), f32),
            pltpu.SemaphoreType.DMA((7, 2)),
        ],
        compiler_params=pltpu.CompilerParams(vmem_limit_bytes=48 * 1024 * 1024),
    )(stale, g, weight, moment, second, lg, rg, lb, rb)


def local(
    activations, out_grads, weight, moment, second, left_gram, right_gram, left_basis, right_basis,
    slot_map, stale_mark,
):
    gradient = gradient_sums(slot_map[0], activations, out_grads)
    outs = state_step(
        gradient, weight[0, 0], moment[0, 0], second[0, 0], left_gram[0, 0],
        right_gram[0, 0], left_basis[0, 0], right_basis[0, 0], stale_mark[0],
    )
    return tuple(item[None, None] for item in outs)


def solution(mesh):
    rows = P("dp", "blk")
    block = P("dp", "blk", None, None, None)
    marks = P("dp", "blk", None)
    return jax.shard_map(
        local,
        mesh=mesh,
        in_specs=(rows, rows) + (block,) * 7 + (marks, marks),
        out_specs=(block,) * 7,
        check_vma=False,
    )
```

```python
import jax
import jax.numpy as jnp
from jax import lax
from jax.experimental import pallas as pl
from jax.experimental.pallas import tpu as pltpu
from jax.sharding import PartitionSpec as P

f32 = jnp.float32
bf16 = jnp.bfloat16
MESH = pl.DeviceIdType.MESH


def gradient_kernel(
    slot_hbm, a_ref, g_ref, out_ref, slot_ref, a_own, at_ref, gg_ref, part_ref, pair_send, pair_recv,
    x_send, x_recv, y_send, y_recv, turn_recv, local_sems, a_sems, g_sems, pair_sems, x_sems, y_sems,
    turn_sems,
):
    loads = [
        pltpu.make_async_copy(src, dst, local_sems.at[i])
        for i, (src, dst) in enumerate(
            ((a_ref, a_own), (g_ref, gg_ref.at[0]), (slot_hbm, slot_ref))
        )
    ]
    for load in loads:
        load.start()
    dp, blk = lax.axis_index("dp"), lax.axis_index("blk")
    x, core = lax.div(dp, 2), lax.rem(dp, 2)
    y, z = lax.div(blk, 8), lax.rem(blk, 8)

    def device(x_to, core_to, y_to, z_to):
        return (x_to * 2 + core_to, y_to * 8 + z_to)

    z_right = device(x, core, y, lax.rem(z + 1, 8))
    z_left = device(x, core, y, lax.rem(z + 7, 8))
    y_far = [None] + [device(x, core, lax.rem(y + 4 - s, 4), z) for s in (1, 2, 3)]
    x_far = [None] + [device(lax.rem(x + e, 4), core, y, z) for e in (1, 2, 3)]
    y_up, y_down = y_far[3], y_far[1]
    other_core = device(x, 1 - core, y, z)

    barrier = pltpu.get_barrier_semaphore()
    for partner in (z_right, z_left, other_core, *y_far[1:], *x_far[1:]):
        pl.semaphore_signal(barrier, inc=1, device_id=partner, device_id_type=MESH)
    pl.semaphore_wait(barrier, 9)

    def remote(src, dst, sems, index, to):
        return pltpu.make_async_remote_copy(
            src_ref=src, dst_ref=dst, send_sem=sems.at[(0, *index)], recv_sem=sems.at[(1, *index)],
            device_id=to, device_id_type=MESH,
        )

    def g_copy(way, step, half):
        rows = pl.ds(half * 512, 512)
        src = g_ref.at[rows] if step == 0 else gg_ref.at[(1, 3)[way], rows]
        slot = ((1, 2), (3, 2))[way][step]
        return remote(src, gg_ref.at[slot, rows], g_sems, (way, step, half), (y_up, y_down)[way])

    def a_copy(way, step, half):
        rows = pl.ds(half * 64, 64)
        src_slot = step if way == 0 else (8 - step) % 8
        dst_slot = step + 1 if way == 0 else 7 - step
        return remote(
            at_ref.at[src_slot, rows], at_ref.at[dst_slot, rows], a_sems, (way, step, half),
            (z_right, z_left)[way],
        )

    def pass_on_a(step, half):
        for way in (0, 1):
            a_copy(way, step - 1, half).wait_recv()
            if step < 3 or half == way:
                a_copy(way, step, half).start()

    def product(s, low, high):
        lhs = at_ref[low:high].reshape((high - low) * 128, 1024)
        got = jnp.dot(lhs, gg_ref[s], preferred_element_type=f32)
        for r in range(low, high):
            part_ref[(0, 1, 3, 2)[s], lax.rem(z + 8 - r, 8)] = got[(r - low) * 128 : (r - low + 1) * 128]

    near, far = (0, 1, 3), (2,)
    place = (0, 1, 3, 2)

    def column(r):
        return lax.rem(z + 8 - r, 8)

    def mine(r):
        return lax.div(column(r), 4) == core

    def places(group):
        return pl.ds(0, 3) if group is near else pl.ds(3, 1)

    def quarter(e):
        return pl.ds(pl.multiple_of(lax.rem(x + e, 4) * 32, 32), 32)

    def pair_copy(u, group):
        at = places(group)
        return remote(
            pair_send.at[u, at], pair_recv.at[u, at], pair_sems, (u, int(group is far)), other_core
        )

    def x_copy(u, e, group):
        at = places(group)
        return remote(
            x_send.at[u, e, at], x_recv.at[u, e, at], x_sems, (u, e, int(group is far)), x_far[e]
        )

    def y_copy(u, s):
        return remote(y_send.at[u, place[s]], y_recv.at[u, s], y_sems, (u, s), y_far[s])

    def turn_copy(u, e):
        return remote(
            y_recv.at[u, lax.rem(x + 4 + e - y, 4)], turn_recv.at[lax.rem(z + 8 - u, 4), quarter(0)],
            turn_sems, (u, e), x_far[e],
        )

    def share(r, group):
        @pl.when(jnp.logical_not(mine(r)))
        def _():
            at = places(group)
            pair_send[r % 4, at] = part_ref[at, column(r)].astype(bf16)
            pair_copy(r % 4, group).start()

    def spread(r, group):
        u, at = r % 4, places(group)

        @pl.when(mine(r))
        def _():
            pair_copy(u, group).wait_recv()
            for e in (2, 1, 3):
                total = part_ref[at, column(r), quarter(e)] + pair_recv[u, at, quarter(e)].astype(f32)
                x_send[u, e, at] = total.astype(bf16)
                x_copy(u, e, group).start()

    def merge(r, group):
        u, at = r % 4, places(group)

        @pl.when(mine(r))
        def _():
            total = part_ref[at, column(r), quarter(0)] + pair_recv[u, at, quarter(0)].astype(f32)
            for e in (1, 3, 2):
                x_copy(u, e, group).wait_recv()
                total = total + x_recv[u, e, at].astype(f32)
            y_send[u, at] = total.astype(bf16)
            for s in group:
                if s:
                    y_copy(u, s).start()
                else:
                    y_recv[u, 0] = y_send[u, 0]

    def cross(r):
        u = r % 4

        @pl.when(mine(r))
        def _():
            for s in (1, 3, 2):
                y_copy(u, s).wait_recv()
            for e in (2, 1, 3):
                turn_copy(u, e).start()
            turn_recv[lax.rem(z + 8 - u, 4), quarter(0)] = y_recv[u, lax.rem(x + 4 - y, 4)]

    for way in (0, 1):
        g_copy(way, 0, way).start()
    loads[0].wait()
    at_ref[0] = a_own[...].T
    for half in (0, 1):
        for way in (0, 1):
            a_copy(way, 0, half).start()
    for way in (0, 1):
        g_copy(way, 0, 1 - way).start()
    loads[1].wait()
    product(0, 0, 1)
    pass_on_a(1, 0)
    for way in (0, 1):
        g_copy(way, 0, way).wait_recv()
        g_copy(way, 1, way).start()
    pass_on_a(1, 1)
    product(0, 1, 2)
    product(0, 7, 8)
    pass_on_a(2, 0)
    for way in (0, 1):
        g_copy(way, 0, 1 - way).wait_recv()
    for s in (1, 3):
        product(s, 0, 2)
        product(s, 7, 8)
    for r in (0, 1, 7):
        share(r, near)
    pass_on_a(2, 1)
    for s in near:
        product(s, 2, 3)
        product(s, 6, 7)
    for r in (2, 6):
        share(r, near)
    for r in (0, 1, 7, 2, 6):
        spread(r, near)
    pass_on_a(3, 0)
    pass_on_a(3, 1)
    for s in near:
        product(s, 3, 4)
        product(s, 5, 6)
    for r in (3, 5):
        share(r, near)
    for way in (0, 1):
        g_copy(way, 1, way).wait_recv()
    product(2, 0, 4)
    product(2, 5, 8)
    for r in (0, 1, 7, 2, 6, 3, 5):
        share(r, far)
    for r in (3, 5):
        spread(r, near)
    for r in (0, 1, 7, 2, 6, 3, 5):
        spread(r, far)
    for r in (0, 1, 7, 2, 6):
        merge(r, near)
    for way in (0, 1):
        a_copy(way, 3, way).wait_recv()
    for s in near:
        product(s, 4, 5)
    share(4, near)
    product(2, 4, 5)
    share(4, far)
    for r in (0, 1, 7, 2, 6):
        merge(r, far)
    spread(4, near)
    spread(4, far)
    for r in (3, 5):
        merge(r, near)
        merge(r, far)
    for r in (0, 1, 7, 2, 6):
        cross(r)
    merge(4, near)
    merge(4, far)
    for r in (3, 5, 4):
        cross(r)

    for way in (0, 1):
        for half in (0, 1):
            g_copy(way, 0, half).wait_send()
            for step in (0, 1, 2):
                a_copy(way, step, half).wait_send()
        g_copy(way, 1, way).wait_send()
        a_copy(way, 3, way).wait_send()
    for u in range(4):
        for group in (near, far):
            pair_copy(u, group).wait_send()
            for e in (1, 2, 3):
                x_copy(u, e, group).wait_send()
        for e in (1, 2, 3):
            y_copy(u, e).wait_send()
            turn_copy(u, e).wait()
    loads[2].wait()
    for j in (0, 1):
        out_ref[j] = turn_recv[pl.ds(slot_ref[0, j] * 2, 2)].reshape(256, 256).astype(f32)


def gradient_sums(slot_map, activations, out_grads):
    vm = pl.BlockSpec(memory_space=pltpu.VMEM)
    hbm = pl.BlockSpec(memory_space=pltpu.HBM)
    dma = pltpu.SemaphoreType.DMA
    return pl.pallas_call(
        gradient_kernel,
        out_shape=jax.ShapeDtypeStruct((2, 256, 256), f32),
        in_specs=[hbm] * 3,
        out_specs=vm,
        scratch_shapes=[
            pltpu.SMEM((1, 2), jnp.int32),
            pltpu.VMEM((1024, 128), bf16),
            pltpu.VMEM((8, 128, 1024), bf16),
            pltpu.VMEM((4, 1024, 256), bf16),
            pltpu.VMEM((4, 8, 128, 256), f32),
            pltpu.VMEM((4, 4, 128, 256), bf16),
            pltpu.VMEM((4, 4, 128, 256), bf16),
            pltpu.VMEM((4, 4, 4, 32, 256), bf16),
            pltpu.VMEM((4, 4, 4, 32, 256), bf16),
            pltpu.VMEM((4, 4, 32, 256), bf16),
            pltpu.VMEM((4, 4, 32, 256), bf16),
            pltpu.VMEM((4, 128, 256), bf16),
            dma((3,)),
            dma((2, 2, 4, 2)),
            dma((2, 2, 2, 2)),
            dma((2, 4, 2)),
            dma((2, 4, 4, 2)),
            dma((2, 4, 4)),
            dma((2, 4, 4)),
        ],
        compiler_params=pltpu.CompilerParams(
            collective_id=0, has_side_effects=True, vmem_limit_bytes=40 * 1024 * 1024
        ),
        cost_estimate=pl.CostEstimate(flops=2 * 1024**3, bytes_accessed=1 << 20, transcendentals=0),
    )(*[pltpu.with_memory_space_constraint(item, pltpu.HBM) for item in (slot_map, activations, out_grads)])


highest = lax.Precision.HIGHEST
beta_one = 0.9
beta_two = 0.95
gram_beta = 0.95
eps_adam = 1e-08
learn_rate = 0.1
decay_rate = 0.01
bias_one = 1.0 - 0.9**10
bias_two = 1.0 - 0.95**10

NB = 32
GROUP = 8


def dot(a, b, ca=1, cb=0, precision=highest):
    return lax.dot_general(
        a, b, (((ca,), (cb,)), ((), ())), precision=precision, preferred_element_type=f32
    )


def split2(x):
    h = x.astype(bf16)
    return h, (x - h.astype(f32)).astype(bf16)


def dot3(a, b, ca=1, cb=0):
    return dot(
        jnp.concatenate([a[0], a[0], a[1]], axis=ca),
        jnp.concatenate([b[0], b[1], b[0]], axis=cb),
        ca, cb, None,
    )


def split3(x):
    h = x.astype(bf16)
    r = x - h.astype(f32)
    m = r.astype(bf16)
    l = (r - m.astype(f32)).astype(bf16)
    return h, m, l


def inverse_factors(a):
    lane = lax.broadcasted_iota(jnp.int32, (NB, 128), 1)
    row = lax.broadcasted_iota(jnp.int32, (NB, 128), 0)
    e = jnp.where(lane % NB == row, 1.0, 0.0).astype(f32)
    pivots = []
    done_e = []
    for b in range(NB // GROUP):
        rows = NB - b * GROUP
        lane_b = lax.broadcasted_iota(jnp.int32, (rows, 128), 1)
        row_b = lax.broadcasted_iota(jnp.int32, (rows, 128), 0)
        base = lane_b - lane_b % NB
        v = [
            jnp.take_along_axis(a, base + (b * GROUP + j), axis=1)
            for j in range(GROUP)
        ]
        for k in range(GROUP):
            piv = v[k][k : k + 1, :]
            pivots.append(piv)
            rec = 1.0 / piv
            m = jnp.where(row_b > k, v[k] * rec, 0.0)
            for j in range(k + 1, GROUP):
                v[j] = v[j] - m * v[j][k : k + 1, :]
            a = a - m * a[k : k + 1, :]
            e = e - m * e[k : k + 1, :]
        done_e.append(e[:GROUP])
        a = a[GROUP:]
        e = e[GROUP:]
    scale = lax.rsqrt(jnp.concatenate(pivots, axis=0))
    return jnp.concatenate(done_e, axis=0) * scale


def stacked_dot(lhs, rhs, ca, cb):
    h, m, l = split3(lhs)
    first = jnp.concatenate([h, h, m, m, h, l], axis=ca)
    h, m, l = split3(rhs)
    return dot(first, jnp.concatenate([h, m, h, m, l, h], axis=cb), ca, cb, None)


def refresh_all(w_ref, z_ref, beside):
    lane = lax.broadcasted_iota(jnp.int32, (NB, 128), 1)
    big_lane = lax.broadcasted_iota(jnp.int32, (128, 128), 1)
    big_row = lax.broadcasted_iota(jnp.int32, (128, 128), 0)
    for tile in range(2):
        c0 = tile * 128
        held = []
        for i in range(4):
            p = tile * 4 + i
            beside[p]()
            packed = None
            for t in range(4):
                x = w_ref[p, t * NB : (t + 1) * NB, c0 : c0 + 128]
                shift = ((t - i) * NB) % 128
                if shift:
                    x = pltpu.roll(x, shift, 1)
                packed = x if packed is None else jnp.where(lane // NB == t, x, packed)
            inv = inverse_factors(packed)
            bd = jnp.where(
                big_lane // NB == big_row // NB, jnp.concatenate([inv] * 4, axis=0), 0.0
            )
            r = stacked_dot(bd, w_ref[p, :, c0:], 1, 0)
            held.append(r)
            for t in range(4):
                z_ref[t, p * NB : (p + 1) * NB, :] = r[t * NB : (t + 1) * NB, 256 - c0 :]
            if i == 3:
                break
            for t in range(4):
                h, m, l = split3(r[t * NB : (t + 1) * NB])
                lhs = jnp.concatenate([h, h, m, m, h, l], axis=0)[:, :128].T[(i + 1) * NB :]
                rhs = jnp.concatenate([h, m, h, m, l, h], axis=0)
                u = dot(lhs, rhs, 1, 0, None)
                for q in range(i + 1, 4):
                    at = (q - i - 1) * NB
                    w_ref[tile * 4 + q, t * NB : (t + 1) * NB, c0:] -= u[at : at + NB]
        if tile == 0:
            for t in range(4):
                rows = jnp.concatenate([r[t * NB : (t + 1) * NB, 128:] for r in held], axis=0)
                u = stacked_dot(rows[:, :128], rows, 0, 0)
                for q in range(4):
                    w_ref[4 + q, t * NB : (t + 1) * NB, 128:] -= u[q * NB : (q + 1) * NB]


def state_kernel(
    stale_ref, g_ref, weight_ref, moment_ref, second_ref, lg_ref, rg_ref, lb_ref, rb_ref,
    weight_hbm, moment_hbm, second_hbm, left_hbm, right_hbm, lb_hbm, rb_hbm,
    weight_out, moment_out, second_out, left_out, right_out, lb_out, rb_out, w_ref, z_ref, sems,
):
    results = (weight_hbm, moment_hbm, second_hbm, left_hbm, right_hbm, lb_hbm, rb_hbm)

    def store(k, i, src):
        return pltpu.make_async_copy(src.at[i], results[k].at[i], sems.at[k, i])

    coef = (1.0 - gram_beta) / 256
    for i in range(2):
        g = g_ref[i]
        rows, columns = split2(g), split2(g.T)
        left_out[i] = gram_beta * lg_ref[i] + coef * dot3(rows, rows, 1, 1)
        right_out[i] = gram_beta * rg_ref[i] + coef * dot3(columns, columns, 1, 1)
        store(3, i, left_out).start()
        store(4, i, right_out).start()

    def weight_steps(i):
        held = {}

        def rotate_left():
            g = g_ref[i]
            moment_new = beta_one * moment_ref[i] + (1.0 - beta_one) * g
            moment_out[i] = moment_new
            store(1, i, moment_out).start()
            both = split2(jnp.concatenate([g, moment_new], axis=1))
            held["half"] = dot3(split2(lb_ref[i].T), both)

        def rotate_right():
            half = held.pop("half")
            both = split2(jnp.concatenate([half[:, :256], half[:, 256:]], axis=0))
            turned = dot3(both, split2(rb_ref[i]))
            rotated, turned = turned[:256], turned[256:]
            second_new = beta_two * second_ref[i] + (1.0 - beta_two) * rotated * rotated
            second_out[i] = second_new
            store(2, i, second_out).start()
            held["normal"] = turned / bias_one / (jnp.sqrt(second_new / bias_two) + eps_adam)

        def back_left():
            held["back"] = dot3(split2(lb_ref[i]), split2(held.pop("normal")))

        def back_right():
            update = dot3(split2(held.pop("back")), split2(rb_ref[i]), 1, 1)
            wide = weight_ref[i].astype(f32)
            weight_out[i] = (wide - learn_rate * (update + decay_rate * wide)).astype(bf16)
            store(0, i, weight_out).start()

        return [rotate_left, rotate_right, back_left, back_right]

    @pl.when(stale_ref[0, 0] > 0)
    def _():
        for i in range(2):
            for side, (s_ref, b_ref) in enumerate(((left_out, lb_ref), (right_out, rb_ref))):
                t = i * 2 + side
                z = dot3(split2(b_ref[i].T), split2(s_ref[i]))
                c = stacked_dot(z, z, 1, 1)
                for p in range(256 // NB):
                    w_ref[p, t * NB : (t + 1) * NB, :256] = c[p * NB : (p + 1) * NB]
                    w_ref[p, t * NB : (t + 1) * NB, 256:] = z[p * NB : (p + 1) * NB]
        refresh_all(w_ref, z_ref, weight_steps(0) + weight_steps(1))
        for i in range(2):
            lb_out[i] = z_ref[i * 2].T
            store(5, i, lb_out).start()
            rb_out[i] = z_ref[i * 2 + 1].T
            store(6, i, rb_out).start()

    @pl.when(stale_ref[0, 0] <= 0)
    def _():
        for i in range(2):
            store(5, i, lb_ref).start()
            store(6, i, rb_ref).start()
            for step in weight_steps(i):
                step()

    for k, src in enumerate((weight_out, moment_out, second_out, left_out, right_out, lb_out, rb_out)):
        for i in range(2):
            store(k, i, src).wait()


def state_step(g, weight, moment, second, lg, rg, lb, rb, stale):
    shape = (2, 256, 256)
    block = jax.ShapeDtypeStruct(shape, f32)
    vm = pl.BlockSpec(memory_space=pltpu.VMEM)
    sm = pl.BlockSpec(memory_space=pltpu.SMEM)
    return pl.pallas_call(
        state_kernel,
        out_shape=(jax.ShapeDtypeStruct(shape, bf16),) + (block,) * 6,
        in_specs=[sm] + [vm] * 8,
        out_specs=[pl.BlockSpec(memory_space=pltpu.HBM)] * 7,
        scratch_shapes=[pltpu.VMEM(shape, bf16)]
        + [pltpu.VMEM(shape, f32)] * 6
        + [
            pltpu.VMEM((8, 4 * NB, 512), f32),
            pltpu.VMEM((4, 256, 256), f32),
            pltpu.SemaphoreType.DMA((7, 2)),
        ],
        compiler_params=pltpu.CompilerParams(vmem_limit_bytes=48 * 1024 * 1024),
    )(stale, g, weight, moment, second, lg, rg, lb, rb)


def local(
    activations, out_grads, weight, moment, second, left_gram, right_gram, left_basis, right_basis,
    slot_map, stale_mark,
):
    gradient = gradient_sums(slot_map[0], activations, out_grads)
    outs = state_step(
        gradient, weight[0, 0], moment[0, 0], second[0, 0], left_gram[0, 0],
        right_gram[0, 0], left_basis[0, 0], right_basis[0, 0], stale_mark[0],
    )
    return tuple(item[None, None] for item in outs)


def solution(mesh):
    rows = P("dp", "blk")
    block = P("dp", "blk", None, None, None)
    marks = P("dp", "blk", None)
    return jax.shard_map(
        local,
        mesh=mesh,
        in_specs=(rows, rows) + (block,) * 7 + (marks, marks),
        out_specs=(block,) * 7,
        check_vma=False,
    )
```

```python
import jax
import jax.numpy as jnp
from jax import lax
from jax.experimental import pallas as pl
from jax.experimental.pallas import tpu as pltpu
from jax.sharding import PartitionSpec as P

f32 = jnp.float32
bf16 = jnp.bfloat16
MESH = pl.DeviceIdType.MESH


def gradient_kernel(
    slot_hbm, a_ref, g_ref, out_ref, slot_ref, a_own, at_ref, gg_ref, part_ref, pair_send, pair_recv,
    x_send, x_recv, y_send, y_recv, turn_recv, local_sems, a_sems, g_sems, pair_sems, x_sems, y_sems,
    turn_sems,
):
    loads = [
        pltpu.make_async_copy(src, dst, local_sems.at[i])
        for i, (src, dst) in enumerate(
            ((a_ref, a_own), (g_ref, gg_ref.at[0]), (slot_hbm, slot_ref))
        )
    ]
    for load in loads:
        load.start()
    dp, blk = lax.axis_index("dp"), lax.axis_index("blk")
    x, core = lax.div(dp, 2), lax.rem(dp, 2)
    y, z = lax.div(blk, 8), lax.rem(blk, 8)

    def device(x_to, core_to, y_to, z_to):
        return (x_to * 2 + core_to, y_to * 8 + z_to)

    z_right = device(x, core, y, lax.rem(z + 1, 8))
    z_left = device(x, core, y, lax.rem(z + 7, 8))
    y_far = [None] + [device(x, core, lax.rem(y + 4 - s, 4), z) for s in (1, 2, 3)]
    x_far = [None] + [device(lax.rem(x + e, 4), core, y, z) for e in (1, 2, 3)]
    y_up, y_down = y_far[3], y_far[1]
    other_core = device(x, 1 - core, y, z)

    barrier = pltpu.get_barrier_semaphore()
    for partner in (z_right, z_left, other_core, *y_far[1:], *x_far[1:]):
        pl.semaphore_signal(barrier, inc=1, device_id=partner, device_id_type=MESH)
    pl.semaphore_wait(barrier, 9)

    def remote(src, dst, sems, index, to):
        return pltpu.make_async_remote_copy(
            src_ref=src, dst_ref=dst, send_sem=sems.at[(0, *index)], recv_sem=sems.at[(1, *index)],
            device_id=to, device_id_type=MESH,
        )

    def g_copy(way, step, half):
        rows = pl.ds(half * 512, 512)
        src = g_ref.at[rows] if step == 0 else gg_ref.at[(1, 3)[way], rows]
        slot = ((1, 2), (3, 2))[way][step]
        return remote(src, gg_ref.at[slot, rows], g_sems, (way, step, half), (y_up, y_down)[way])

    def a_copy(way, step, half):
        rows = pl.ds(half * 64, 64)
        src_slot = step if way == 0 else (8 - step) % 8
        dst_slot = step + 1 if way == 0 else 7 - step
        return remote(
            at_ref.at[src_slot, rows], at_ref.at[dst_slot, rows], a_sems, (way, step, half),
            (z_right, z_left)[way],
        )

    def pass_on_a(step, half):
        for way in (0, 1):
            a_copy(way, step - 1, half).wait_recv()
            if step < 3 or half == way:
                a_copy(way, step, half).start()

    def product(s, low, high):
        lhs = at_ref[low:high].reshape((high - low) * 128, 1024)
        got = jnp.dot(lhs, gg_ref[s], preferred_element_type=f32)
        for r in range(low, high):
            part_ref[(0, 1, 3, 2)[s], lax.rem(z + 8 - r, 8)] = got[(r - low) * 128 : (r - low + 1) * 128]

    near, far = (0, 1, 3), (2,)
    place = (0, 1, 3, 2)

    def column(r):
        return lax.rem(z + 8 - r, 8)

    def mine(r):
        return lax.div(column(r), 4) == core

    def places(group):
        return pl.ds(0, 3) if group is near else pl.ds(3, 1)

    def quarter(e):
        return pl.ds(pl.multiple_of(lax.rem(x + e, 4) * 32, 32), 32)

    def pair_copy(u, group):
        at = places(group)
        return remote(
            pair_send.at[u, at], pair_recv.at[u, at], pair_sems, (u, int(group is far)), other_core
        )

    def x_copy(u, e, group):
        at = places(group)
        return remote(
            x_send.at[u, e, at], x_recv.at[u, e, at], x_sems, (u, e, int(group is far)), x_far[e]
        )

    def y_copy(u, s):
        return remote(y_send.at[u, place[s]], y_recv.at[u, s], y_sems, (u, s), y_far[s])

    def turn_copy(u, s):
        e = lax.rem(y + 4 + s - x, 4)
        return pltpu.make_async_remote_copy(
            src_ref=y_recv.at[u, s], dst_ref=turn_recv.at[lax.rem(z + 8 - u, 4), quarter(0)],
            send_sem=turn_sems.at[0, u, s], recv_sem=turn_sems.at[1, u, e],
            device_id=device(lax.rem(y + s, 4), core, y, z), device_id_type=MESH,
        )

    def turn_arrival(u, e):
        return remote(
            y_recv.at[u, 0], turn_recv.at[lax.rem(z + 8 - u, 4), quarter(4 - e)], turn_sems, (u, e), x_far[1]
        )

    def share(r, group):
        @pl.when(jnp.logical_not(mine(r)))
        def _():
            at = places(group)
            pair_send[r % 4, at] = part_ref[at, column(r)].astype(bf16)
            pair_copy(r % 4, group).start()

    def spread(r, group):
        u, at = r % 4, places(group)

        @pl.when(mine(r))
        def _():
            pair_copy(u, group).wait_recv()
            for e in (2, 1, 3):
                total = part_ref[at, column(r), quarter(e)] + pair_recv[u, at, quarter(e)].astype(f32)
                x_send[u, e, at] = total.astype(bf16)
                x_copy(u, e, group).start()

    def merge(r, group):
        u, at = r % 4, places(group)

        @pl.when(mine(r))
        def _():
            total = part_ref[at, column(r), quarter(0)] + pair_recv[u, at, quarter(0)].astype(f32)
            for e in (1, 3, 2):
                x_copy(u, e, group).wait_recv()
                total = total + x_recv[u, e, at].astype(f32)
            y_send[u, at] = total.astype(bf16)
            for s in group:
                if s:
                    y_copy(u, s).start()
                else:
                    y_recv[u, 0] = y_send[u, 0]

    def cross(r, group):
        u = r % 4

        @pl.when(mine(r))
        def _():
            for s in group:
                if s:
                    y_copy(u, s).wait_recv()

                @pl.when(x != lax.rem(y + s, 4))
                def _():
                    turn_copy(u, s).start()

                @pl.when(x == lax.rem(y + s, 4))
                def _():
                    turn_recv[lax.rem(z + 8 - u, 4), quarter(0)] = y_recv[u, s]

    for way in (0, 1):
        g_copy(way, 0, way).start()
    loads[0].wait()
    at_ref[0] = a_own[...].T
    for half in (0, 1):
        for way in (0, 1):
            a_copy(way, 0, half).start()
    for way in (0, 1):
        g_copy(way, 0, 1 - way).start()
    loads[1].wait()
    product(0, 0, 1)
    pass_on_a(1, 0)
    pass_on_a(1, 1)
    product(0, 1, 2)
    product(0, 7, 8)
    pass_on_a(2, 0)
    for way in (0, 1):
        g_copy(way, 0, way).wait_recv()
        g_copy(way, 0, 1 - way).wait_recv()
        g_copy(way, 1, way).start()
    for s in (1, 3):
        product(s, 0, 2)
        product(s, 7, 8)
    for r in (0, 1, 7):
        share(r, near)
    pass_on_a(2, 1)
    for s in near:
        product(s, 2, 3)
        product(s, 6, 7)
    for r in (2, 6):
        share(r, near)
    for r in (0, 1, 7, 2, 6):
        spread(r, near)
    pass_on_a(3, 0)
    pass_on_a(3, 1)
    for s in near:
        product(s, 3, 4)
        product(s, 5, 6)
    for r in (3, 5):
        share(r, near)
    for way in (0, 1):
        g_copy(way, 1, way).wait_recv()
    product(2, 0, 4)
    product(2, 5, 8)
    for r in (0, 1, 7, 2, 6, 3, 5):
        share(r, far)
    for r in (3, 5):
        spread(r, near)
    for r in (0, 1, 7, 2, 6, 3, 5):
        spread(r, far)
    for r in (0, 1, 7, 2, 6):
        merge(r, near)
    for way in (0, 1):
        a_copy(way, 3, way).wait_recv()
    for s in near:
        product(s, 4, 5)
    share(4, near)
    product(2, 4, 5)
    share(4, far)
    for r in (0, 1, 7, 2, 6):
        cross(r, near)
    spread(4, near)
    spread(4, far)
    for r in (3, 5):
        merge(r, near)
    for r in (0, 1, 7, 2, 6, 3, 5):
        merge(r, far)
    for r in (3, 5):
        cross(r, near)
    merge(4, near)
    merge(4, far)
    for r in (0, 1, 7, 2, 6, 3, 5):
        cross(r, far)
    cross(4, near)
    cross(4, far)

    for way in (0, 1):
        for half in (0, 1):
            g_copy(way, 0, half).wait_send()
            for step in (0, 1, 2):
                a_copy(way, step, half).wait_send()
        g_copy(way, 1, way).wait_send()
        a_copy(way, 3, way).wait_send()
    for u in range(4):
        for group in (near, far):
            pair_copy(u, group).wait_send()
            for e in (1, 2, 3):
                x_copy(u, e, group).wait_send()
        for e in (1, 2, 3):
            y_copy(u, e).wait_send()
            turn_arrival(u, e).wait_recv()
        for s in range(4):

            @pl.when(x != lax.rem(y + s, 4))
            def _():
                turn_copy(u, s).wait_send()

    loads[2].wait()
    for j in (0, 1):
        out_ref[j] = turn_recv[pl.ds(slot_ref[0, j] * 2, 2)].reshape(256, 256).astype(f32)


def gradient_sums(slot_map, activations, out_grads):
    vm = pl.BlockSpec(memory_space=pltpu.VMEM)
    hbm = pl.BlockSpec(memory_space=pltpu.HBM)
    dma = pltpu.SemaphoreType.DMA
    return pl.pallas_call(
        gradient_kernel,
        out_shape=jax.ShapeDtypeStruct((2, 256, 256), f32),
        in_specs=[hbm] * 3,
        out_specs=vm,
        scratch_shapes=[
            pltpu.SMEM((1, 2), jnp.int32),
            pltpu.VMEM((1024, 128), bf16),
            pltpu.VMEM((8, 128, 1024), bf16),
            pltpu.VMEM((4, 1024, 256), bf16),
            pltpu.VMEM((4, 8, 128, 256), f32),
            pltpu.VMEM((4, 4, 128, 256), bf16),
            pltpu.VMEM((4, 4, 128, 256), bf16),
            pltpu.VMEM((4, 4, 4, 32, 256), bf16),
            pltpu.VMEM((4, 4, 4, 32, 256), bf16),
            pltpu.VMEM((4, 4, 32, 256), bf16),
            pltpu.VMEM((4, 4, 32, 256), bf16),
            pltpu.VMEM((4, 128, 256), bf16),
            dma((3,)),
            dma((2, 2, 4, 2)),
            dma((2, 2, 2, 2)),
            dma((2, 4, 2)),
            dma((2, 4, 4, 2)),
            dma((2, 4, 4)),
            dma((2, 4, 4)),
        ],
        compiler_params=pltpu.CompilerParams(
            collective_id=0, has_side_effects=True, vmem_limit_bytes=40 * 1024 * 1024
        ),
        cost_estimate=pl.CostEstimate(flops=2 * 1024**3, bytes_accessed=1 << 20, transcendentals=0),
    )(*[pltpu.with_memory_space_constraint(item, pltpu.HBM) for item in (slot_map, activations, out_grads)])


highest = lax.Precision.HIGHEST
beta_one = 0.9
beta_two = 0.95
gram_beta = 0.95
eps_adam = 1e-08
learn_rate = 0.1
decay_rate = 0.01
bias_one = 1.0 - 0.9**10
bias_two = 1.0 - 0.95**10

NB = 32
GROUP = 16


def dot(a, b, ca=1, cb=0, precision=highest):
    return lax.dot_general(
        a, b, (((ca,), (cb,)), ((), ())), precision=precision, preferred_element_type=f32
    )


def split2(x):
    h = x.astype(bf16)
    return h, (x - h.astype(f32)).astype(bf16)


def dot3(a, b, ca=1, cb=0):
    return dot(
        jnp.concatenate([a[0], a[0], a[1]], axis=ca),
        jnp.concatenate([b[0], b[1], b[0]], axis=cb),
        ca, cb, None,
    )


def split3(x):
    h = x.astype(bf16)
    r = x - h.astype(f32)
    m = r.astype(bf16)
    l = (r - m.astype(f32)).astype(bf16)
    return h, m, l


def inverse_factors(a):
    lane = lax.broadcasted_iota(jnp.int32, (NB, 128), 1)
    row = lax.broadcasted_iota(jnp.int32, (NB, 128), 0)
    e = jnp.where(lane % NB == row, 1.0, 0.0).astype(f32)
    pivots = []
    done_e = []
    for b in range(NB // GROUP):
        rows = NB - b * GROUP
        lane_b = lax.broadcasted_iota(jnp.int32, (rows, 128), 1)
        row_b = lax.broadcasted_iota(jnp.int32, (rows, 128), 0)
        base = lane_b - lane_b % NB
        v = [
            jnp.take_along_axis(a, base + (b * GROUP + j), axis=1)
            for j in range(GROUP)
        ]
        for k in range(GROUP):
            piv = v[k][k : k + 1, :]
            pivots.append(piv)
            rec = 1.0 / piv
            m = jnp.where(row_b > k, v[k] * rec, 0.0)
            for j in range(k + 1, GROUP):
                v[j] = v[j] - m * v[j][k : k + 1, :]
            a = a - m * a[k : k + 1, :]
            e = e - m * e[k : k + 1, :]
        done_e.append(e[:GROUP])
        a = a[GROUP:]
        e = e[GROUP:]
    scale = lax.rsqrt(jnp.concatenate(pivots, axis=0))
    return jnp.concatenate(done_e, axis=0) * scale


def stacked_dot(lhs, rhs, ca, cb):
    h, m, l = split3(lhs)
    first = jnp.concatenate([h, h, m, m, h, l], axis=ca)
    h, m, l = split3(rhs)
    return dot(first, jnp.concatenate([h, m, h, m, l, h], axis=cb), ca, cb, None)


def refresh_all(w_ref, z_ref, beside):
    lane = lax.broadcasted_iota(jnp.int32, (NB, 128), 1)
    big_lane = lax.broadcasted_iota(jnp.int32, (128, 128), 1)
    big_row = lax.broadcasted_iota(jnp.int32, (128, 128), 0)
    for tile in range(2):
        c0 = tile * 128
        held = []
        for i in range(4):
            p = tile * 4 + i
            beside[p]()
            packed = None
            for t in range(4):
                x = w_ref[p, t * NB : (t + 1) * NB, c0 : c0 + 128]
                shift = ((t - i) * NB) % 128
                if shift:
                    x = pltpu.roll(x, shift, 1)
                packed = x if packed is None else jnp.where(lane // NB == t, x, packed)
            inv = inverse_factors(packed)
            bd = jnp.where(
                big_lane // NB == big_row // NB, jnp.concatenate([inv] * 4, axis=0), 0.0
            )
            r = stacked_dot(bd, w_ref[p, :, c0:], 1, 0)
            held.append(r)
            for t in range(4):
                z_ref[t, p * NB : (p + 1) * NB, :] = r[t * NB : (t + 1) * NB, 256 - c0 :]
            if i == 3:
                break
            for t in range(4):
                h, m, l = split3(r[t * NB : (t + 1) * NB])
                lhs = jnp.concatenate([h, h, m, m, h, l], axis=0)[:, :128].T[(i + 1) * NB :]
                rhs = jnp.concatenate([h, m, h, m, l, h], axis=0)
                u = dot(lhs, rhs, 1, 0, None)
                for q in range(i + 1, 4):
                    at = (q - i - 1) * NB
                    w_ref[tile * 4 + q, t * NB : (t + 1) * NB, c0:] -= u[at : at + NB]
        if tile == 0:
            for t in range(4):
                rows = jnp.concatenate([r[t * NB : (t + 1) * NB, 128:] for r in held], axis=0)
                u = stacked_dot(rows[:, :128], rows, 0, 0)
                for q in range(4):
                    w_ref[4 + q, t * NB : (t + 1) * NB, 128:] -= u[q * NB : (q + 1) * NB]


def state_kernel(
    stale_ref, g_ref, weight_ref, moment_ref, second_ref, lg_ref, rg_ref, lb_ref, rb_ref,
    weight_hbm, moment_hbm, second_hbm, left_hbm, right_hbm, lb_hbm, rb_hbm,
    weight_out, moment_out, second_out, left_out, right_out, lb_out, rb_out, w_ref, z_ref, sems,
):
    results = (weight_hbm, moment_hbm, second_hbm, left_hbm, right_hbm, lb_hbm, rb_hbm)

    def store(k, i, src):
        return pltpu.make_async_copy(src.at[i], results[k].at[i], sems.at[k, i])

    coef = (1.0 - gram_beta) / 256
    for i in range(2):
        g = g_ref[i]
        rows, columns = split2(g), split2(g.T)
        left_out[i] = gram_beta * lg_ref[i] + coef * dot3(rows, rows, 1, 1)
        right_out[i] = gram_beta * rg_ref[i] + coef * dot3(columns, columns, 1, 1)
        store(3, i, left_out).start()
        store(4, i, right_out).start()

    def weight_steps(i):
        held = {}

        def rotate_left():
            g = g_ref[i]
            moment_new = beta_one * moment_ref[i] + (1.0 - beta_one) * g
            moment_out[i] = moment_new
            store(1, i, moment_out).start()
            both = split2(jnp.concatenate([g, moment_new], axis=1))
            held["half"] = dot3(split2(lb_ref[i].T), both)

        def rotate_right():
            half = held.pop("half")
            both = split2(jnp.concatenate([half[:, :256], half[:, 256:]], axis=0))
            turned = dot3(both, split2(rb_ref[i]))
            rotated, turned = turned[:256], turned[256:]
            second_new = beta_two * second_ref[i] + (1.0 - beta_two) * rotated * rotated
            second_out[i] = second_new
            store(2, i, second_out).start()
            held["normal"] = turned / bias_one / (jnp.sqrt(second_new / bias_two) + eps_adam)

        def back_left():
            held["back"] = dot3(split2(lb_ref[i]), split2(held.pop("normal")))

        def back_right():
            update = dot3(split2(held.pop("back")), split2(rb_ref[i]), 1, 1)
            wide = weight_ref[i].astype(f32)
            weight_out[i] = (wide - learn_rate * (update + decay_rate * wide)).astype(bf16)
            store(0, i, weight_out).start()

        return [rotate_left, rotate_right, back_left, back_right]

    @pl.when(stale_ref[0, 0] > 0)
    def _():
        for i in range(2):
            for side, (s_ref, b_ref) in enumerate(((left_out, lb_ref), (right_out, rb_ref))):
                t = i * 2 + side
                z = dot3(split2(b_ref[i].T), split2(s_ref[i]))
                c = stacked_dot(z, z, 1, 1)
                for p in range(256 // NB):
                    w_ref[p, t * NB : (t + 1) * NB, :256] = c[p * NB : (p + 1) * NB]
                    w_ref[p, t * NB : (t + 1) * NB, 256:] = z[p * NB : (p + 1) * NB]
        refresh_all(w_ref, z_ref, weight_steps(0) + weight_steps(1))
        for i in range(2):
            lb_out[i] = z_ref[i * 2].T
            store(5, i, lb_out).start()
            rb_out[i] = z_ref[i * 2 + 1].T
            store(6, i, rb_out).start()

    @pl.when(stale_ref[0, 0] <= 0)
    def _():
        for i in range(2):
            store(5, i, lb_ref).start()
            store(6, i, rb_ref).start()
            for step in weight_steps(i):
                step()

    for k, src in enumerate((weight_out, moment_out, second_out, left_out, right_out, lb_out, rb_out)):
        for i in range(2):
            store(k, i, src).wait()


def state_step(g, weight, moment, second, lg, rg, lb, rb, stale):
    shape = (2, 256, 256)
    block = jax.ShapeDtypeStruct(shape, f32)
    vm = pl.BlockSpec(memory_space=pltpu.VMEM)
    sm = pl.BlockSpec(memory_space=pltpu.SMEM)
    return pl.pallas_call(
        state_kernel,
        out_shape=(jax.ShapeDtypeStruct(shape, bf16),) + (block,) * 6,
        in_specs=[sm] + [vm] * 8,
        out_specs=[pl.BlockSpec(memory_space=pltpu.HBM)] * 7,
        scratch_shapes=[pltpu.VMEM(shape, bf16)]
        + [pltpu.VMEM(shape, f32)] * 6
        + [
            pltpu.VMEM((8, 4 * NB, 512), f32),
            pltpu.VMEM((4, 256, 256), f32),
            pltpu.SemaphoreType.DMA((7, 2)),
        ],
        compiler_params=pltpu.CompilerParams(vmem_limit_bytes=48 * 1024 * 1024),
    )(stale, g, weight, moment, second, lg, rg, lb, rb)


def local(
    activations, out_grads, weight, moment, second, left_gram, right_gram, left_basis, right_basis,
    slot_map, stale_mark,
):
    gradient = gradient_sums(slot_map[0], activations, out_grads)
    outs = state_step(
        gradient, weight[0, 0], moment[0, 0], second[0, 0], left_gram[0, 0],
        right_gram[0, 0], left_basis[0, 0], right_basis[0, 0], stale_mark[0],
    )
    return tuple(item[None, None] for item in outs)


def solution(mesh):
    rows = P("dp", "blk")
    block = P("dp", "blk", None, None, None)
    marks = P("dp", "blk", None)
    return jax.shard_map(
        local,
        mesh=mesh,
        in_specs=(rows, rows) + (block,) * 7 + (marks, marks),
        out_specs=(block,) * 7,
        check_vma=False,
    )
```

```python
import jax
import jax.numpy as jnp
from jax import lax
from jax.experimental import pallas as pl
from jax.experimental.pallas import tpu as pltpu
from jax.sharding import PartitionSpec as P

f32 = jnp.float32
bf16 = jnp.bfloat16
MESH = pl.DeviceIdType.MESH


def gradient_kernel(
    slot_hbm, a_ref, g_ref, out_ref, slot_ref, a_own, at_ref, gg_ref, part_ref, pair_send, pair_recv,
    x_send, x_recv, y_send, y_recv, turn_recv, local_sems, a_sems, g_sems, pair_sems, x_sems, y_sems,
    turn_sems,
):
    loads = [
        pltpu.make_async_copy(src, dst, local_sems.at[i])
        for i, (src, dst) in enumerate(
            ((a_ref, a_own), (g_ref, gg_ref.at[0]), (slot_hbm, slot_ref))
        )
    ]
    for load in loads:
        load.start()
    dp, blk = lax.axis_index("dp"), lax.axis_index("blk")
    x, core = lax.div(dp, 2), lax.rem(dp, 2)
    y, z = lax.div(blk, 8), lax.rem(blk, 8)

    def device(x_to, core_to, y_to, z_to):
        return (x_to * 2 + core_to, y_to * 8 + z_to)

    z_right = device(x, core, y, lax.rem(z + 1, 8))
    z_left = device(x, core, y, lax.rem(z + 7, 8))
    y_far = [None] + [device(x, core, lax.rem(y + 4 - s, 4), z) for s in (1, 2, 3)]
    x_far = [None] + [device(lax.rem(x + e, 4), core, y, z) for e in (1, 2, 3)]
    y_up, y_down = y_far[3], y_far[1]
    other_core = device(x, 1 - core, y, z)

    barrier = pltpu.get_barrier_semaphore()
    for partner in (z_right, z_left, other_core, *y_far[1:], *x_far[1:]):
        pl.semaphore_signal(barrier, inc=1, device_id=partner, device_id_type=MESH)
    pl.semaphore_wait(barrier, 9)

    def remote(src, dst, sems, index, to):
        return pltpu.make_async_remote_copy(
            src_ref=src, dst_ref=dst, send_sem=sems.at[(0, *index)], recv_sem=sems.at[(1, *index)],
            device_id=to, device_id_type=MESH,
        )

    def g_copy(way, step, half):
        rows = pl.ds(half * 512, 512)
        src = g_ref.at[rows] if step == 0 else gg_ref.at[(1, 3)[way], rows]
        slot = ((1, 2), (3, 2))[way][step]
        return remote(src, gg_ref.at[slot, rows], g_sems, (way, step, half), (y_up, y_down)[way])

    def a_copy(way, step, half):
        rows = pl.ds(half * 64, 64)
        src_slot = step if way == 0 else (8 - step) % 8
        dst_slot = step + 1 if way == 0 else 7 - step
        return remote(
            at_ref.at[src_slot, rows], at_ref.at[dst_slot, rows], a_sems, (way, step, half),
            (z_right, z_left)[way],
        )

    def pass_on_a(step, half):
        for way in (0, 1):
            a_copy(way, step - 1, half).wait_recv()
            if step < 3 or half == way:
                a_copy(way, step, half).start()

    def product(s, low, high):
        lhs = at_ref[low:high].reshape((high - low) * 128, 1024)
        got = jnp.dot(lhs, gg_ref[s], preferred_element_type=f32)
        for r in range(low, high):
            part_ref[(0, 1, 3, 2)[s], lax.rem(z + 8 - r, 8)] = got[(r - low) * 128 : (r - low + 1) * 128]

    near, far = (0, 1, 3), (2,)
    place = (0, 1, 3, 2)

    def column(r):
        return lax.rem(z + 8 - r, 8)

    def mine(r):
        return lax.div(column(r), 4) == core

    def places(group):
        return pl.ds(0, 3) if group is near else pl.ds(3, 1)

    def quarter(e):
        return pl.ds(pl.multiple_of(lax.rem(x + e, 4) * 32, 32), 32)

    def pair_copy(u, group):
        at = places(group)
        return remote(
            pair_send.at[u, at], pair_recv.at[u, at], pair_sems, (u, int(group is far)), other_core
        )

    def x_copy(u, e, group):
        at = places(group)
        return remote(
            x_send.at[u, e, at], x_recv.at[u, e, at], x_sems, (u, e, int(group is far)), x_far[e]
        )

    def y_copy(u, s):
        return remote(y_send.at[u, place[s]], y_recv.at[u, s], y_sems, (u, s), y_far[s])

    def turn_copy(u, s):
        e = lax.rem(y + 4 + s - x, 4)
        return pltpu.make_async_remote_copy(
            src_ref=y_recv.at[u, s], dst_ref=turn_recv.at[lax.rem(z + 8 - u, 4), quarter(0)],
            send_sem=turn_sems.at[0, u, s], recv_sem=turn_sems.at[1, u, e],
            device_id=device(lax.rem(y + s, 4), core, y, z), device_id_type=MESH,
        )

    def turn_arrival(u, e):
        return remote(
            y_recv.at[u, 0], turn_recv.at[lax.rem(z + 8 - u, 4), quarter(4 - e)], turn_sems, (u, e), x_far[1]
        )

    def share(r, group):
        @pl.when(jnp.logical_not(mine(r)))
        def _():
            at = places(group)
            pair_send[r % 4, at] = part_ref[at, column(r)].astype(bf16)
            pair_copy(r % 4, group).start()

    def spread(r, group):
        u, at = r % 4, places(group)

        @pl.when(mine(r))
        def _():
            pair_copy(u, group).wait_recv()
            for e in (2, 1, 3):
                total = part_ref[at, column(r), quarter(e)] + pair_recv[u, at, quarter(e)].astype(f32)
                x_send[u, e, at] = total.astype(bf16)
                x_copy(u, e, group).start()

    def merge(r, group):
        u, at = r % 4, places(group)

        @pl.when(mine(r))
        def _():
            total = part_ref[at, column(r), quarter(0)] + pair_recv[u, at, quarter(0)].astype(f32)
            for e in (1, 3, 2):
                x_copy(u, e, group).wait_recv()
                total = total + x_recv[u, e, at].astype(f32)
            y_send[u, at] = total.astype(bf16)
            for s in group:
                if s:
                    y_copy(u, s).start()
                else:
                    y_recv[u, 0] = y_send[u, 0]

    def cross(r, group):
        u = r % 4

        @pl.when(mine(r))
        def _():
            for s in group:
                if s:
                    y_copy(u, s).wait_recv()

                @pl.when(x != lax.rem(y + s, 4))
                def _():
                    turn_copy(u, s).start()

                @pl.when(x == lax.rem(y + s, 4))
                def _():
                    turn_recv[lax.rem(z + 8 - u, 4), quarter(0)] = y_recv[u, s]

    for way in (0, 1):
        g_copy(way, 0, way).start()
    loads[0].wait()
    at_ref[0] = a_own[...].T
    for half in (0, 1):
        for way in (0, 1):
            a_copy(way, 0, half).start()
    for way in (0, 1):
        g_copy(way, 0, 1 - way).start()
    loads[1].wait()
    product(0, 0, 1)
    pass_on_a(1, 0)
    pass_on_a(1, 1)
    product(0, 1, 2)
    product(0, 7, 8)
    pass_on_a(2, 0)
    for way in (0, 1):
        g_copy(way, 0, way).wait_recv()
        g_copy(way, 0, 1 - way).wait_recv()
        g_copy(way, 1, way).start()
    for s in (1, 3):
        product(s, 0, 2)
        product(s, 7, 8)
    for r in (0, 1, 7):
        share(r, near)
    pass_on_a(2, 1)
    for s in near:
        product(s, 2, 3)
        product(s, 6, 7)
    for r in (2, 6):
        share(r, near)
    for r in (0, 1, 7, 2, 6):
        spread(r, near)
    pass_on_a(3, 0)
    pass_on_a(3, 1)
    for s in near:
        product(s, 3, 4)
        product(s, 5, 6)
    for r in (3, 5):
        share(r, near)
    for way in (0, 1):
        g_copy(way, 1, way).wait_recv()
    product(2, 0, 4)
    product(2, 5, 8)
    for r in (0, 1, 7, 2, 6, 3, 5):
        share(r, far)
    for r in (3, 5):
        spread(r, near)
    for r in (0, 1, 7, 2, 6, 3, 5):
        spread(r, far)
    for r in (0, 1, 7, 2, 6):
        merge(r, near)
    for way in (0, 1):
        a_copy(way, 3, way).wait_recv()
    for s in near:
        product(s, 4, 5)
    share(4, near)
    product(2, 4, 5)
    share(4, far)
    for r in (3, 5):
        merge(r, near)
    spread(4, near)
    spread(4, far)
    for r in (0, 1, 7, 2, 6):
        cross(r, near)
    for r in (0, 1, 7, 2, 6, 3, 5):
        merge(r, far)
    for r in (3, 5):
        cross(r, near)
    merge(4, near)
    merge(4, far)
    for r in (0, 1, 7, 2, 6, 3, 5):
        cross(r, far)
    cross(4, near)
    cross(4, far)

    for way in (0, 1):
        for half in (0, 1):
            g_copy(way, 0, half).wait_send()
            for step in (0, 1, 2):
                a_copy(way, step, half).wait_send()
        g_copy(way, 1, way).wait_send()
        a_copy(way, 3, way).wait_send()
    for u in range(4):
        for group in (near, far):
            pair_copy(u, group).wait_send()
            for e in (1, 2, 3):
                x_copy(u, e, group).wait_send()
        for e in (1, 2, 3):
            y_copy(u, e).wait_send()
            turn_arrival(u, e).wait_recv()
        for s in range(4):

            @pl.when(x != lax.rem(y + s, 4))
            def _():
                turn_copy(u, s).wait_send()

    loads[2].wait()
    for j in (0, 1):
        out_ref[j] = turn_recv[pl.ds(slot_ref[0, j] * 2, 2)].reshape(256, 256).astype(f32)


def gradient_sums(slot_map, activations, out_grads):
    vm = pl.BlockSpec(memory_space=pltpu.VMEM)
    hbm = pl.BlockSpec(memory_space=pltpu.HBM)
    dma = pltpu.SemaphoreType.DMA
    return pl.pallas_call(
        gradient_kernel,
        out_shape=jax.ShapeDtypeStruct((2, 256, 256), f32),
        in_specs=[hbm] * 3,
        out_specs=vm,
        scratch_shapes=[
            pltpu.SMEM((1, 2), jnp.int32),
            pltpu.VMEM((1024, 128), bf16),
            pltpu.VMEM((8, 128, 1024), bf16),
            pltpu.VMEM((4, 1024, 256), bf16),
            pltpu.VMEM((4, 8, 128, 256), f32),
            pltpu.VMEM((4, 4, 128, 256), bf16),
            pltpu.VMEM((4, 4, 128, 256), bf16),
            pltpu.VMEM((4, 4, 4, 32, 256), bf16),
            pltpu.VMEM((4, 4, 4, 32, 256), bf16),
            pltpu.VMEM((4, 4, 32, 256), bf16),
            pltpu.VMEM((4, 4, 32, 256), bf16),
            pltpu.VMEM((4, 128, 256), bf16),
            dma((3,)),
            dma((2, 2, 4, 2)),
            dma((2, 2, 2, 2)),
            dma((2, 4, 2)),
            dma((2, 4, 4, 2)),
            dma((2, 4, 4)),
            dma((2, 4, 4)),
        ],
        compiler_params=pltpu.CompilerParams(
            collective_id=0, has_side_effects=True, vmem_limit_bytes=40 * 1024 * 1024
        ),
        cost_estimate=pl.CostEstimate(flops=2 * 1024**3, bytes_accessed=1 << 20, transcendentals=0),
    )(*[pltpu.with_memory_space_constraint(item, pltpu.HBM) for item in (slot_map, activations, out_grads)])


highest = lax.Precision.HIGHEST
beta_one = 0.9
beta_two = 0.95
gram_beta = 0.95
eps_adam = 1e-08
learn_rate = 0.1
decay_rate = 0.01
bias_one = 1.0 - 0.9**10
bias_two = 1.0 - 0.95**10

NB = 32
GROUP = 16


def dot(a, b, ca=1, cb=0, precision=highest):
    return lax.dot_general(
        a, b, (((ca,), (cb,)), ((), ())), precision=precision, preferred_element_type=f32
    )


def split2(x):
    h = x.astype(bf16)
    return h, (x - h.astype(f32)).astype(bf16)


def dot3(a, b, ca=1, cb=0):
    return dot(
        jnp.concatenate([a[0], a[0], a[1]], axis=ca),
        jnp.concatenate([b[0], b[1], b[0]], axis=cb),
        ca, cb, None,
    )


def split3(x):
    h = x.astype(bf16)
    r = x - h.astype(f32)
    m = r.astype(bf16)
    l = (r - m.astype(f32)).astype(bf16)
    return h, m, l


def inverse_factors(a):
    lane = lax.broadcasted_iota(jnp.int32, (NB, 128), 1)
    row = lax.broadcasted_iota(jnp.int32, (NB, 128), 0)
    e = jnp.where(lane % NB == row, 1.0, 0.0).astype(f32)
    pivots = []
    done_e = []
    for b in range(NB // GROUP):
        rows = NB - b * GROUP
        lane_b = lax.broadcasted_iota(jnp.int32, (rows, 128), 1)
        row_b = lax.broadcasted_iota(jnp.int32, (rows, 128), 0)
        base = lane_b - lane_b % NB
        v = [
            jnp.take_along_axis(a, base + (b * GROUP + j), axis=1)
            for j in range(GROUP)
        ]
        for k in range(GROUP):
            piv = v[k][k : k + 1, :]
            pivots.append(piv)
            rec = 1.0 / piv
            m = jnp.where(row_b > k, v[k] * rec, 0.0)
            for j in range(k + 1, GROUP):
                v[j] = v[j] - m * v[j][k : k + 1, :]
            a = a - m * a[k : k + 1, :]
            e = e - m * e[k : k + 1, :]
        done_e.append(e[:GROUP])
        a = a[GROUP:]
        e = e[GROUP:]
    scale = lax.rsqrt(jnp.concatenate(pivots, axis=0))
    return jnp.concatenate(done_e, axis=0) * scale


def stacked_dot(lhs, rhs, ca, cb):
    h, m, l = split3(lhs)
    first = jnp.concatenate([h, h, m, m, h, l], axis=ca)
    h, m, l = split3(rhs)
    return dot(first, jnp.concatenate([h, m, h, m, l, h], axis=cb), ca, cb, None)


def refresh_all(w_ref, z_ref, beside):
    lane = lax.broadcasted_iota(jnp.int32, (NB, 128), 1)
    big_lane = lax.broadcasted_iota(jnp.int32, (128, 128), 1)
    big_row = lax.broadcasted_iota(jnp.int32, (128, 128), 0)
    for tile in range(2):
        c0 = tile * 128
        held = []
        for i in range(4):
            p = tile * 4 + i
            beside[p]()
            packed = None
            for t in range(4):
                x = w_ref[p, t * NB : (t + 1) * NB, c0 : c0 + 128]
                shift = ((t - i) * NB) % 128
                if shift:
                    x = pltpu.roll(x, shift, 1)
                packed = x if packed is None else jnp.where(lane // NB == t, x, packed)
            inv = inverse_factors(packed)
            bd = jnp.where(
                big_lane // NB == big_row // NB, jnp.concatenate([inv] * 4, axis=0), 0.0
            )
            r = stacked_dot(bd, w_ref[p, :, c0:], 1, 0)
            held.append(r)
            for t in range(4):
                z_ref[t, p * NB : (p + 1) * NB, :] = r[t * NB : (t + 1) * NB, 256 - c0 :]
            if i == 3:
                break
            for t in range(4):
                h, m, l = split3(r[t * NB : (t + 1) * NB])
                lhs = jnp.concatenate([h, h, m, m, h, l], axis=0)[:, :128].T[(i + 1) * NB :]
                rhs = jnp.concatenate([h, m, h, m, l, h], axis=0)
                u = dot(lhs, rhs, 1, 0, None)
                for q in range(i + 1, 4):
                    at = (q - i - 1) * NB
                    w_ref[tile * 4 + q, t * NB : (t + 1) * NB, c0:] -= u[at : at + NB]
        if tile == 0:
            for t in range(4):
                rows = jnp.concatenate([r[t * NB : (t + 1) * NB, 128:] for r in held], axis=0)
                u = stacked_dot(rows[:, :128], rows, 0, 0)
                for q in range(4):
                    w_ref[4 + q, t * NB : (t + 1) * NB, 128:] -= u[q * NB : (q + 1) * NB]


def state_kernel(
    stale_ref, g_ref, weight_ref, moment_ref, second_ref, lg_ref, rg_ref, lb_ref, rb_ref,
    weight_hbm, moment_hbm, second_hbm, left_hbm, right_hbm, lb_hbm, rb_hbm,
    weight_out, moment_out, second_out, left_out, right_out, lb_out, rb_out, w_ref, z_ref, sems,
):
    results = (weight_hbm, moment_hbm, second_hbm, left_hbm, right_hbm, lb_hbm, rb_hbm)

    def store(k, i, src):
        return pltpu.make_async_copy(src.at[i], results[k].at[i], sems.at[k, i])

    coef = (1.0 - gram_beta) / 256

    def grams(i):
        g = g_ref[i]
        rows, columns = split2(g), split2(g.T)
        left_out[i] = gram_beta * lg_ref[i] + coef * dot3(rows, rows, 1, 1)
        right_out[i] = gram_beta * rg_ref[i] + coef * dot3(columns, columns, 1, 1)
        store(3, i, left_out).start()
        store(4, i, right_out).start()

    def weight_steps(i):
        held = {}

        def rotate_left():
            g = g_ref[i]
            moment_new = beta_one * moment_ref[i] + (1.0 - beta_one) * g
            moment_out[i] = moment_new
            store(1, i, moment_out).start()
            both = split2(jnp.concatenate([g, moment_new], axis=1))
            held["half"] = dot3(split2(lb_ref[i].T), both)

        def rotate_right():
            half = held.pop("half")
            both = split2(jnp.concatenate([half[:, :256], half[:, 256:]], axis=0))
            turned = dot3(both, split2(rb_ref[i]))
            rotated, turned = turned[:256], turned[256:]
            second_new = beta_two * second_ref[i] + (1.0 - beta_two) * rotated * rotated
            second_out[i] = second_new
            store(2, i, second_out).start()
            held["normal"] = turned / bias_one / (jnp.sqrt(second_new / bias_two) + eps_adam)

        def back_left():
            held["back"] = dot3(split2(lb_ref[i]), split2(held.pop("normal")))

        def back_right():
            update = dot3(split2(held.pop("back")), split2(rb_ref[i]), 1, 1)
            wide = weight_ref[i].astype(f32)
            weight_out[i] = (wide - learn_rate * (update + decay_rate * wide)).astype(bf16)
            store(0, i, weight_out).start()

        return [rotate_left, rotate_right, back_left, back_right]

    @pl.when(stale_ref[0, 0] > 0)
    def _():
        for i in range(2):
            grams(i)
            for side, (s_ref, b_ref) in enumerate(((left_out, lb_ref), (right_out, rb_ref))):
                t = i * 2 + side
                z = dot3(split2(b_ref[i].T), split2(s_ref[i]))
                c = stacked_dot(z, z, 1, 1)
                for p in range(256 // NB):
                    w_ref[p, t * NB : (t + 1) * NB, :256] = c[p * NB : (p + 1) * NB]
                    w_ref[p, t * NB : (t + 1) * NB, 256:] = z[p * NB : (p + 1) * NB]
        refresh_all(w_ref, z_ref, weight_steps(0) + weight_steps(1))
        for i in range(2):
            lb_out[i] = z_ref[i * 2].T
            store(5, i, lb_out).start()
            rb_out[i] = z_ref[i * 2 + 1].T
            store(6, i, rb_out).start()

    @pl.when(stale_ref[0, 0] <= 0)
    def _():
        for i in range(2):
            grams(i)
            store(5, i, lb_ref).start()
            store(6, i, rb_ref).start()
            for step in weight_steps(i):
                step()

    for k, src in enumerate((weight_out, moment_out, second_out, left_out, right_out, lb_out, rb_out)):
        for i in range(2):
            store(k, i, src).wait()


def state_step(g, weight, moment, second, lg, rg, lb, rb, stale):
    shape = (2, 256, 256)
    block = jax.ShapeDtypeStruct(shape, f32)
    vm = pl.BlockSpec(memory_space=pltpu.VMEM)
    sm = pl.BlockSpec(memory_space=pltpu.SMEM)
    return pl.pallas_call(
        state_kernel,
        out_shape=(jax.ShapeDtypeStruct(shape, bf16),) + (block,) * 6,
        in_specs=[sm] + [vm] * 8,
        out_specs=[pl.BlockSpec(memory_space=pltpu.HBM)] * 7,
        scratch_shapes=[pltpu.VMEM(shape, bf16)]
        + [pltpu.VMEM(shape, f32)] * 6
        + [
            pltpu.VMEM((8, 4 * NB, 512), f32),
            pltpu.VMEM((4, 256, 256), f32),
            pltpu.SemaphoreType.DMA((7, 2)),
        ],
        compiler_params=pltpu.CompilerParams(vmem_limit_bytes=48 * 1024 * 1024),
    )(stale, g, weight, moment, second, lg, rg, lb, rb)


def local(
    activations, out_grads, weight, moment, second, left_gram, right_gram, left_basis, right_basis,
    slot_map, stale_mark,
):
    gradient = gradient_sums(slot_map[0], activations, out_grads)
    outs = state_step(
        gradient, weight[0, 0], moment[0, 0], second[0, 0], left_gram[0, 0],
        right_gram[0, 0], left_basis[0, 0], right_basis[0, 0], stale_mark[0],
    )
    return tuple(item[None, None] for item in outs)


def solution(mesh):
    rows = P("dp", "blk")
    block = P("dp", "blk", None, None, None)
    marks = P("dp", "blk", None)
    return jax.shard_map(
        local,
        mesh=mesh,
        in_specs=(rows, rows) + (block,) * 7 + (marks, marks),
        out_specs=(block,) * 7,
        check_vma=False,
    )
```
